256 devices in a mesh: users: 128 (over z, x, y), rep: 2 (over core).
Axes of the slice: x: 4, y: 4, z: 8, core: 2. Of those that a mesh axis runs over, the one named last changes fastest.
Arguments:
- user_factors: float32 [131072, 256], P('users'), may hold values from -1.5 to 1.5
- user_accum: float32 [131072, 256], P('users'), may hold values from 0.5 to 8
- item_factors: float32 [32768, 256], P('users'), may hold values from -1.5 to 1.5
- item_accum: float32 [32768, 256], P('users'), may hold values from 0.5 to 8
- tile_counts: bfloat16 [128, 2, 128, 128, 128], P('users', 'rep'), may hold values from 0 to 20, as said below
- tile_user: int32 [128, 2, 128], P('users', 'rep'), may hold values from 0 to 7
- tile_item: int32 [128, 2, 128], P('users', 'rep'), may hold values from 0 to 255, as said below
- send_list: int32 [128, 2, 128], P('users', 'rep'), may hold values from 0 to 2, as said below
Outputs:
- new_users: float32 [131072, 256], P('users')
- new_user_accum: float32 [131072, 256], P('users')
- new_items: float32 [32768, 256], P('users')
- new_item_accum: float32 [32768, 256], P('users')
The draws below stay inside these ranges and needn't reach their ends.
Inputs may be any that keep to these rules, and one draw needn't show every extreme that they name: `tile_counts`: zero means no interaction. `tile_item`: panel b belongs to owner b // 2. Device (q, r) uses at most one panel of each owner o, namely o * 2 + send_list[o, r, q], and only where send_list[o, r, q] < 2. `send_list`: the value 2 means that requester q uses no panel of owner o.
All inputs are finite; a program needn't handle non-finite values.
Results may differ from the reference program's by a relative error of at most 0.0026.
Values may be sent and summed in bfloat16 or wider, within the bound.
A program may use at most 128 MiB of HBM per device.

```python
import math
import jax
import jax.numpy as jnp
from jax import lax

R = 256
TILE = 128
UB = 8
TILES = 128
IPD = 2
USERS = 131072
ITEMS = 32768
N_USERS = 128
N_REP = 2


def request_table(key):
    base_key = jax.random.fold_in(key, 101)
    kept_slot = jax.random.randint(jax.random.fold_in(base_key, 1), (N_USERS, N_REP, N_USERS), 0, 10) >= 3
    own_slot = jnp.arange(N_USERS)[:, None, None] == jnp.arange(N_USERS)[None, None, :]
    kept_slot = kept_slot | own_slot
    picked = jax.random.randint(jax.random.fold_in(base_key, 2), (N_USERS, N_REP, N_USERS), 0, IPD)
    return jnp.where(kept_slot, picked, IPD).astype(jnp.int32)


def draw_tile_item(key, part):
    table = request_table(key)
    scores = jax.random.randint(jax.random.fold_in(key, 202), (N_USERS, N_REP, TILES, N_USERS), 0, 2 ** 20)
    scores = scores + jnp.where(table < IPD, 2 ** 21, 0)[:, :, None, :]
    owner_pick = jnp.argmax(scores, axis=-1).astype(jnp.int32)
    spread = jnp.broadcast_to(table[:, :, None, :], scores.shape)
    panel_pick = jnp.take_along_axis(spread, owner_pick[..., None], axis=-1)[..., 0]
    return (owner_pick * IPD + panel_pick).astype(jnp.int32)


def draw_send_list(key, part):
    return jnp.transpose(request_table(key), (2, 1, 0)).astype(jnp.int32)


def draw_tile_counts(key, part):
    shape = (N_USERS, N_REP, TILES, TILE, TILE)
    coin = jax.random.uniform(jax.random.fold_in(key, 303), shape, jnp.float32)
    level = jax.random.uniform(jax.random.fold_in(key, 304), shape, jnp.float32)
    nonzero = coin < 0.35
    amounts = jnp.exp(level * jnp.log(20.0))
    return jnp.where(nonzero, amounts, 0.0).astype(jnp.bfloat16)


def plant(entries, stream_key, low, largest):
    index_at = [jax.random.randint(jax.random.fold_in(stream_key, axis), (), 0, length) for axis, length in enumerate(entries.shape)]
    main_axis = entries.shape.index(max(entries.shape))
    beside = index_at[:main_axis] + [(index_at[main_axis] + 1) % entries.shape[main_axis]] + index_at[main_axis + 1:]
    return entries.at[tuple(index_at)].set(low).at[tuple(beside)].set(largest)


def levels(key, dims, split, smallest, top_value):
    gain, own = 1.0, jax.random.fold_in(key, 6)
    for position, shards_of in split:
        heights = jnp.exp(jax.random.uniform(jax.random.fold_in(own, position), (shards_of,), jnp.float32, smallest / len(split), top_value / len(split)))
        gain = gain * jnp.repeat(heights, dims[position] // shards_of).reshape([-1 if axis == position else 1 for axis in range(len(dims))])
    return gain


def gaussian(rng, shape, scale, reach, split=(), kind=jnp.bfloat16):
    array = scale * jax.random.normal(rng, shape, jnp.float32)
    if split:
        array = array * levels(rng, shape, split, -0.22, 0.18)
    return jnp.clip(array, -reach, reach).astype(kind)


def setup_inputs(seed: int = 0) -> dict:
    keys = jax.random.split(jax.random.key(seed), 9)
    user_factors = gaussian(keys[0], (USERS, R), 0.25, 1.5, ((0, 128),), jnp.float32)
    user_accum = jnp.clip(jnp.exp(math.log(8.0) - 2.7725887 * jax.random.uniform(keys[1], (USERS, R), jnp.float32) ** levels(keys[1], (USERS, R), ((0, 128),), -0.2, 0.2)), 0.5, 8.0)
    item_factors = gaussian(keys[2], (ITEMS, R), 0.25, 1.5, ((0, 128),), jnp.float32)
    item_accum = jnp.clip(jnp.exp(math.log(8.0) - 2.7725887 * jax.random.uniform(keys[3], (ITEMS, R), jnp.float32) ** levels(keys[3], (ITEMS, R), ((0, 128),), -0.2, 0.2)), 0.5, 8.0)
    tile_counts = draw_tile_counts(jax.random.fold_in(keys[8], 71), 0)
    tile_user = plant(jax.random.randint(keys[5], (N_USERS, N_REP, TILES), 0, UB), jax.random.fold_in(keys[5], 1), 0, UB - 1).astype(jnp.int32)
    tile_item = draw_tile_item(jax.random.fold_in(keys[8], 71), 0)
    send_list = draw_send_list(jax.random.fold_in(keys[8], 71), 0)
    return {"user_factors": user_factors, "user_accum": user_accum, "item_factors": item_factors, "item_accum": item_accum, "tile_counts": tile_counts, "tile_user": tile_user, "tile_item": tile_item, "send_list": send_list}


CONF_SLOPE = 0.5
ERR_SCALE = 1.0 / 64.0

def tile_terms(user_strip, panels, counts, users_idx, fetch_index, slot_index, slot_count):
    tile_count = counts.shape[0]
    group_size = math.gcd(tile_count, 32)
    group_count = tile_count // group_size
    side = counts.shape[-1]
    width = panels.shape[-1]

    def tile_step(totals, inputs):
        user_total, slot_total = totals
        block_counts, block_user, block_fetch, block_slot = inputs
        user_rows = user_strip[block_user].astype(jnp.float32)
        item_rows = panels[block_fetch].astype(jnp.float32)
        predicted = jnp.einsum('gur,gir->gui', user_rows, item_rows)
        amount = block_counts.astype(jnp.float32)
        confidence = 1.0 + CONF_SLOPE * amount
        preference = jnp.where(amount > 0, 1.0, 0.0).astype(jnp.float32)
        weighted_err = lax.optimization_barrier((confidence * (predicted - preference) * ERR_SCALE).astype(jnp.bfloat16))
        weighted_err = weighted_err.astype(jnp.float32)
        user_part = jnp.einsum('gui,gir->gur', weighted_err, item_rows)
        item_part = jnp.einsum('gui,gur->gir', weighted_err, user_rows)
        user_total = user_total.at[block_user].add(user_part)
        slot_total = slot_total.at[block_slot].add(item_part)
        return ((user_total, slot_total), None)
    start = (jnp.zeros((user_strip.shape[0], side, width), jnp.float32), jnp.zeros((slot_count, side, width), jnp.float32))
    inputs = (counts.reshape(group_count, group_size, side, side), users_idx.reshape(group_count, group_size).astype(jnp.int32), fetch_index.reshape(group_count, group_size).astype(jnp.int32), slot_index.reshape(group_count, group_size).astype(jnp.int32))
    (user_total, slot_total), _ = lax.scan(tile_step, start, inputs)
    return (user_total, slot_total)

def reference(user_factors, user_accum, item_factors, item_accum, tile_counts, tile_user, tile_item, send_list):
    strips = user_factors.astype(jnp.bfloat16).reshape(N_USERS, UB, TILE, R)
    panels = item_factors.astype(jnp.bfloat16).reshape(N_USERS * IPD, TILE, R)

    def per_strip(item_grad, inputs):
        user_strip, counts, users_idx, items_idx, strip_index = inputs
        user_grad = jnp.zeros((UB, TILE, R), jnp.float32)
        for rep_index in range(N_REP):
            user_part, slot_part = tile_terms(user_strip, panels, counts[rep_index], users_idx[rep_index], items_idx[rep_index], items_idx[rep_index] // IPD, N_USERS)
            user_grad = user_grad + user_part
            rounded = lax.optimization_barrier(slot_part.astype(jnp.bfloat16)).astype(jnp.float32)
            panel_of = send_list[:, rep_index, strip_index]
            target = jnp.arange(N_USERS, dtype=jnp.int32) * IPD + jnp.minimum(panel_of, IPD - 1).astype(jnp.int32)
            item_grad = item_grad.at[target].add(rounded)
        return (item_grad, user_grad)
    item_grad, user_grads = lax.scan(per_strip, jnp.zeros((N_USERS * IPD, TILE, R), jnp.float32), (strips, tile_counts, tile_user, tile_item, jnp.arange(N_USERS, dtype=jnp.int32)))
    user_grad = user_grads.reshape(USERS, R)
    item_grad = item_grad.reshape(ITEMS, R)
    new_user_accum = user_accum + user_grad * user_grad
    new_users = user_factors - user_grad / jnp.sqrt(new_user_accum)
    new_item_accum = item_accum + item_grad * item_grad
    new_items = item_factors - item_grad / jnp.sqrt(new_item_accum)
    return (new_users, new_user_accum, new_items, new_item_accum)
```

```python
import heapq

import jax
import jax.numpy as jnp
from jax import lax
from jax.experimental import pallas as pl
from jax.experimental.pallas import tpu as pltpu
from jax.sharding import PartitionSpec as P

MESH = pl.DeviceIdType.MESH
AXES = ("z", "x", "y")
SIZE = {"z": 8, "x": 4, "y": 4}
STREAMS = (
    (slice(0, 2), 48, 16, ("x", "y", "z")),
    (slice(0, 1), 0, 48, ("y", "z", "x")),
    (slice(1, 2), 0, 48, ("x", "z", "y")),
)
HOP, RATE, PAIR_RATE = 1.7, 50e3, 500e3


def ring_steps(n):
    out = []
    for d in range(n // 2):
        for s in (1, -1):
            last = d == n // 2 - 1
            out.append((s, d, ((0,) if s == 1 else (1,)) if last else (0, 1)))
    return out


def gather_plan():
    sends = {}
    for i, (ksel, row0, rows, order) in enumerate(STREAMS):
        a, b, c = order
        unit = (ksel.stop - ksel.start) * rows * 128 * 2
        na, nb, nc = SIZE[a], SIZE[b], SIZE[c]
        p1 = [(i, 1, 0, s, d) for s, d, h in ring_steps(na)]
        for s, d, h in ring_steps(na):
            deps = [] if d == 0 else [(i, 1, 0, s, d - 1)]
            sends[(i, 1, 0, s, d)] = dict(axis=a, s=s, h=h, deps=deps, size=unit * len(h), at={a: -s * d, b: 0, c: 0})
        for s, d, h in ring_steps(nb):
            deps = p1 if d == 0 else [(i, 2, 0, s, d - 1)]
            sends[(i, 2, 0, s, d)] = dict(axis=b, s=s, h=h, deps=deps, size=unit * len(h) * na, at={a: None, b: -s * d, c: 0})
        for j in range(nb):
            off = j if j <= nb // 2 else j - nb
            if off == 0:
                line = p1
            elif abs(off) == nb // 2:
                line = [(i, 2, 0, 1, nb // 2 - 1), (i, 2, 0, -1, nb // 2 - 1)]
            else:
                line = [(i, 2, 0, -1 if off > 0 else 1, abs(off) - 1)]
            for s, d, h in ring_steps(nc):
                deps = line if d == 0 else [(i, 3, j, s, d - 1)]
                sends[(i, 3, j, s, d)] = dict(axis=c, s=s, h=h, deps=deps, size=unit * len(h) * na, at={a: None, b: off, c: -s * d})
    for i, (ksel, row0, rows, order) in enumerate(STREAMS):
        a, b, c = order
        unit = (ksel.stop - ksel.start) * rows * 256 * 2
        nb, nc = SIZE[b], SIZE[c]
        for m in range(nc):
            off = m if m <= nc // 2 else m - nc
            if off == 0:
                deps = [k for k in sends if k[0] == i and k[1] in (1, 2)]
            elif abs(off) == nc // 2:
                deps = [(i, 3, j, s, nc // 2 - 1) for j in range(nb) for s in (1, -1)]
            else:
                deps = [(i, 3, j, -1 if off > 0 else 1, abs(off) - 1) for j in range(nb)]
            sends[(i, 4, m, 0, 0)] = dict(axis="pair", s=0, h=(0, 1), deps=deps, size=unit * 128 // nc, at={a: None, b: None, c: off})
    arrive, start, free = {}, {}, {}
    pending = dict(sends)
    heap = []
    waiting = {k: set(v["deps"]) for k, v in sends.items()}
    users = {}
    for k, v in sends.items():
        for dep in v["deps"]:
            users.setdefault(dep, []).append(k)
        if not v["deps"]:
            heapq.heappush(heap, (0.0, k))
    while heap:
        t, k = heapq.heappop(heap)
        v = sends[k]
        link = (v["axis"], v["s"])
        begin = max(t, free.get(link, 0.0))
        rate = PAIR_RATE if v["axis"] == "pair" else RATE
        end = begin + v["size"] / rate
        free[link] = end
        start[k] = t
        arrive[k] = end + (0.5 if v["axis"] == "pair" else HOP)
        for q in users.get(k, ()):
            waiting[q].discard(k)
            if not waiting[q]:
                heapq.heappush(heap, (max(arrive[x] for x in sends[q]["deps"]), q))
    order = sorted(sends, key=lambda k: (start[k], k))
    return sends, order, arrive, free


def wrap(v, n):
    return lax.rem(v + 2 * n, n)


def coords():
    u = lax.axis_index("users")
    return {"z": u // 16, "x": lax.rem(u // 4, 4), "y": lax.rem(u, 4)}


def index_of(c):
    return c["z"] * 16 + c["x"] * 4 + c["y"]


def neighbour(me, axis, s):
    c = dict(me)
    c[axis] = wrap(me[axis] + s, SIZE[axis])
    return index_of(c)


def greet(me, rep):
    bar = pltpu.get_barrier_semaphore()
    for axis in AXES:
        for s in (1, -1):
            pl.semaphore_signal(bar, inc=1, device_id=(neighbour(me, axis, s), rep), device_id_type=MESH)
    pl.semaphore_signal(bar, inc=1, device_id=(index_of(me), 1 - rep), device_id_type=MESH)
    pl.semaphore_wait(bar, 7)


SENDS, ORDER, ARRIVE, FREE = gather_plan()
INDEX = {k: n for n, k in enumerate(ORDER)}


def gather_kernel(own_ref, items_ref, out_ref, other_items_ref, half, send, recv, local):
    me = coords()
    rep = lax.axis_index("rep")
    half[...] = own_ref[...].reshape(2, 128, 256).astype(jnp.bfloat16)
    lines = pl.ds(pl.multiple_of(rep * 64, 64), 64)
    keep = pltpu.make_async_copy(half.at[:, lines], out_ref.at[me["z"], me["x"], me["y"], :, lines], local)
    keep.start()
    greet(me, rep)

    def window(key):
        v = SENDS[key]
        ksel, row0, rows, order = STREAMS[key[0]]
        where = []
        for axis in AXES:
            off = v["at"][axis]
            where.append(slice(None) if off is None else wrap(me[axis] + off, SIZE[axis]))
        row = pl.ds(pl.multiple_of(rep * 64 + row0, 16), rows)
        cols = slice(None) if len(v["h"]) == 2 else pl.ds(128 * v["h"][0], 128)
        return tuple(where) + (ksel, row, cols), (ksel, row, cols)

    def copy(key):
        v = SENDS[key]
        place, mine = window(key)
        if key[1] == 4:
            target = (index_of(me), 1 - rep)
        else:
            target = (neighbour(me, v["axis"], v["s"]), rep)
        src = half.at[mine] if key[1] == 1 and not v["deps"] else out_ref.at[place]
        return pltpu.make_async_remote_copy(
            src_ref=src, dst_ref=out_ref.at[place], send_sem=send.at[INDEX[key]], recv_sem=recv.at[INDEX[key]],
            device_id=target, device_id_type=MESH,
        )

    swap = pltpu.make_async_remote_copy(
        src_ref=items_ref, dst_ref=other_items_ref, send_sem=send.at[len(ORDER)], recv_sem=recv.at[len(ORDER)],
        device_id=(index_of(me), 1 - rep), device_id_type=MESH,
    )
    swap.start()
    done = set()
    kept = False
    for key in ORDER:
        for dep in sorted(SENDS[key]["deps"], key=lambda k: ARRIVE[k]):
            if dep not in done:
                copy(dep).wait_recv()
                done.add(dep)
        if SENDS[key]["deps"] and not kept:
            keep.wait()
            kept = True
        copy(key).start()
    for key in sorted(ORDER, key=lambda k: ARRIVE[k]):
        if key not in done:
            copy(key).wait_recv()
    for key in ORDER:
        copy(key).wait_send()
    swap.wait()


def gather_panels(own, items):
    count = len(ORDER) + 1
    return pl.pallas_call(
        gather_kernel,
        out_shape=(
            jax.ShapeDtypeStruct((8, 4, 4, 2, 128, 256), jnp.bfloat16),
            jax.ShapeDtypeStruct(items.shape, items.dtype),
        ),
        in_specs=[pl.BlockSpec(memory_space=pltpu.VMEM), pl.BlockSpec(memory_space=pl.ANY)],
        out_specs=(pl.BlockSpec(memory_space=pl.ANY), pl.BlockSpec(memory_space=pl.ANY)),
        scratch_shapes=[
            pltpu.VMEM((2, 128, 256), jnp.bfloat16),
            pltpu.SemaphoreType.DMA((count,)),
            pltpu.SemaphoreType.DMA((count,)),
            pltpu.SemaphoreType.DMA,
        ],
        name="gather_panels",
        compiler_params=pltpu.CompilerParams(collective_id=0, has_side_effects=True, vmem_limit_bytes=48 * 2**20),
    )(own, items)


def reduce_steps(n):
    out = []
    for q in range(n // 2):
        for s in (1, -1):
            out.append((s, q, n // 2 - q, ((0,) if s == 1 else (1,)) if q == 0 else (0, 1)))
    return out


def far_first(n):
    out = [n // 2]
    for d in range(n // 2 - 1, 0, -1):
        out += [d, -d]
    return out + [0]


def reduce_plan():
    tasks = {}
    zs = far_first(8)
    for n, off in enumerate(zs):
        tasks[("pair", off)] = dict(kind="pair", deps=[], size=16 * 64 * 256 * 2, rank=n)
    allz = [("pair", off) for off in zs]
    for i, (ksel, row0, rows, order) in enumerate(STREAMS):
        a, b, c = order
        na, nb, nc = SIZE[a], SIZE[b], SIZE[c]
        unit = (ksel.stop - ksel.start) * rows * 128 * 2
        for rank, j in enumerate(far_first(nb)):
            def shares(dist_c):
                if b == "z":
                    return [("pair", j if j != -(nb // 2) else nb // 2)]
                if c == "z":
                    return [("pair", dist_c)]
                return allz
            for s, q, e, h in reduce_steps(nc):
                at = s * e
                if at == -(nc // 2):
                    at = nc // 2
                deps = shares(at) + ([("send", i, 1, j, s, q - 1)] if q else [])
                tasks[("send", i, 1, j, s, q)] = dict(kind="send", axis=c, s=s, h=h, deps=deps, size=unit * len(h) * na, rank=rank, e=s * e)
            last = nc // 2 - 1
            tasks[("sum", i, 1, j)] = dict(kind="sum", deps=shares(0) + [("send", i, 1, j, s, last) for s in (1, -1)], size=unit * 2 * na, rank=rank)
        for s, q, e, h in reduce_steps(nb):
            line = s * e if s * e != -(nb // 2) else nb // 2
            deps = [("sum", i, 1, line)] + ([("send", i, 2, 0, s, q - 1)] if q else [])
            tasks[("send", i, 2, 0, s, q)] = dict(kind="send", axis=b, s=s, h=h, deps=deps, size=unit * len(h) * na, rank=-5, e=line)
        tasks[("sum", i, 2)] = dict(kind="sum", deps=[("sum", i, 1, 0)] + [("send", i, 2, 0, s, nb // 2 - 1) for s in (1, -1)], size=unit * 2 * na, rank=-5)
        for s, q, e, h in reduce_steps(na):
            deps = [("sum", i, 2)] + ([("send", i, 3, 0, s, q - 1)] if q else [])
            tasks[("send", i, 3, 0, s, q)] = dict(kind="send", axis=a, s=s, h=h, deps=deps, size=2 * unit * len(h), rank=-9, e=s * e)
        tasks[("sum", i, 3)] = dict(kind="sum", deps=[("sum", i, 2)] + [("send", i, 3, 0, s, na // 2 - 1) for s in (1, -1)], size=unit * 2, rank=-9)
    done_at, free, order = {}, {}, []
    left = dict(tasks)
    for k in [k for k in left if k[0] == "pair"]:
        v = left.pop(k)
        begin = free.get("pair", 0.0)
        free["pair"] = begin + v["size"] / PAIR_RATE
        done_at[k] = free["pair"] + 0.7
        order.append(k)
    now = 0.0
    while left:
        best = None
        for k, v in left.items():
            if all(d in done_at for d in v["deps"]):
                ready = max([done_at[d] for d in v["deps"]])
                link = free.get((v["axis"], v["s"]), 0.0) if v["kind"] == "send" else 0.0
                begin = max(ready, now)
                score = (max(begin, link if link > begin + 2.0 else 0.0), v["rank"], -k[-1] if v["kind"] == "send" else -9)
                if best is None or score < best[0]:
                    best = (score, k, begin)
        _, k, begin = best
        v = left.pop(k)
        now = begin + 0.05 + v["size"] / 900e3
        if v["kind"] == "send":
            link = (v["axis"], v["s"])
            free[link] = max(now, free.get(link, 0.0)) + v["size"] / RATE
            done_at[k] = free[link] + HOP
        else:
            done_at[k] = now
        order.append(k)
    return tasks, order, done_at, free


TASKS, TASK_ORDER, DONE_AT, LINKS = reduce_plan()
SEND_INDEX = {k: n for n, k in enumerate([k for k in TASK_ORDER if k[0] != "sum"])}


def dims(i):
    ksel, row0, rows, order = STREAMS[i]
    return ksel.stop - ksel.start, rows, tuple(SIZE[x] for x in order)


def reduce_kernel(slots_ref, used_ref, user_ref, user_out, grad_out, mine, other, *rest):
    bufs = [dict(zip(("s1", "r1", "l1", "s2", "r2", "l2", "s3", "r3"), rest[8 * i: 8 * i + 8])) for i in range(3)]
    total, send, recv, load, last = rest[24:]
    me = coords()
    rep = lax.axis_index("rep")
    row_mine = pl.multiple_of(rep * 64, 64)
    row_other = pl.multiple_of((1 - rep) * 64, 64)
    zof = {off: wrap(me["z"] + off, 8) for off in range(-4, 5)}
    loads = {}
    for n, off in enumerate(far_first(8)):
        loads[off] = pltpu.make_async_copy(slots_ref.at[zof[off], :, :, pl.ds(row_mine, 64), :], mine.at[zof[off]], load.at[n])
        loads[off].start()
    greet(me, rep)
    pair = (index_of(me), 1 - rep)

    def remote(key):
        if key[0] == "pair":
            z = zof[key[1]]
            return pltpu.make_async_remote_copy(
                src_ref=slots_ref.at[z, :, :, pl.ds(row_other, 64), :], dst_ref=other.at[z],
                send_sem=send.at[SEND_INDEX[key]], recv_sem=recv.at[SEND_INDEX[key]], device_id=pair, device_id_type=MESH)
        _, i, phase, j, s, q = key
        v = TASKS[key]
        nb = dims(i)[2][1]
        cols = pl.ds(0, 256) if len(v["h"]) == 2 else pl.ds(128 * v["h"][0], 128)
        side = 0 if s == 1 else 1
        at = (j % nb, side, q) if phase == 1 else (side, q)
        tail = (slice(None),) * (2 if phase == 3 else 3) + (cols,)
        return pltpu.make_async_remote_copy(
            src_ref=bufs[i]["s%d" % phase].at[at + tail], dst_ref=bufs[i]["r%d" % phase].at[at + tail],
            send_sem=send.at[SEND_INDEX[key]], recv_sem=recv.at[SEND_INDEX[key]],
            device_id=(neighbour(me, v["axis"], s), rep), device_id_type=MESH)

    def share(i, offs, n, cols):
        ksel, row0, rows, order = STREAMS[i]
        a, b, c = order
        where = {b: wrap(me[b] + offs[0], SIZE[b]), c: wrap(me[c] + offs[1], SIZE[c]), a: n}
        owner = index_of(where)
        place = (where["z"], where["x"], where["y"], pl.ds(row0, rows), cols)
        x = mine[place].astype(jnp.float32)
        y = other[place].astype(jnp.float32)
        out = []
        for k in range(ksel.start, ksel.stop):
            ux = used_ref[0, owner * 2 + k] > 0
            uy = used_ref[1, owner * 2 + k] > 0
            out.append(jnp.where(ux, x, 0.0) + jnp.where(uy, y, 0.0))
        return out

    def work(key):
        v = TASKS[key]
        i = key[1]
        kk, rows, (na, nb, nc) = dims(i)
        buf = bufs[i]
        if key[0] == "send":
            _, i, phase, j, s, q = key
            side = 0 if s == 1 else 1
            for h in ((0, 1) if (q == 1) else (None,)):
                cols = pl.ds(128 * h, 128) if h is not None else (pl.ds(0, 256) if len(v["h"]) == 2 else pl.ds(128 * v["h"][0], 128))
                got = q >= 2 or (q == 1 and h == side)

                def body(n, _, cols=cols, got=got):
                    if phase == 1:
                        parts = share(i, (j, v["e"]), n, cols)
                    elif phase == 2:
                        parts = [buf["l1"][v["e"] % nb, n, k, :, cols] for k in range(kk)]
                    for k in range(kk):
                        x = parts[k]
                        if phase == 1:
                            if got:
                                x = x + buf["r1"][j % nb, side, q - 1, n, k, :, cols].astype(jnp.float32)
                            buf["s1"][j % nb, side, q, n, k, :, cols] = x.astype(jnp.bfloat16)
                        else:
                            if got:
                                x = x + buf["r2"][side, q - 1, n, k, :, cols].astype(jnp.float32)
                            buf["s2"][side, q, n, k, :, cols] = x.astype(jnp.bfloat16)
                    return 0

                if phase == 3:
                    n = wrap(me[STREAMS[i][3][0]] + v["e"], na)
                    for k in range(kk):
                        x = buf["l2"][n, k, :, cols]
                        if got:
                            x = x + buf["r3"][side, q - 1, k, :, cols]
                        buf["s3"][side, q, k, :, cols] = x
                else:
                    lax.fori_loop(0, na, body, 0)
            return
        phase = key[2]
        end = {1: nc, 2: nb, 3: na}[phase] // 2 - 1
        full = pl.ds(0, 256)
        if phase == 1:
            j = key[3]

            def body(n, _):
                parts = share(i, (j, 0), n, full)
                for k in range(kk):
                    x = parts[k]
                    for side in range(2):
                        x = x + buf["r1"][j % nb, side, end, n, k].astype(jnp.float32)
                    buf["l1"][j % nb, n, k] = x
                return 0

            lax.fori_loop(0, na, body, 0)
        elif phase == 2:

            def body(n, _):
                for k in range(kk):
                    x = buf["l1"][0, n, k]
                    for side in range(2):
                        x = x + buf["r2"][side, end, n, k].astype(jnp.float32)
                    buf["l2"][n, k] = x
                return 0

            lax.fori_loop(0, na, body, 0)
        else:
            ksel, row0, rows, order = STREAMS[i]
            n = me[order[0]]
            for k in range(kk):
                x = buf["l2"][n, k]
                for side in range(2):
                    x = x + buf["r3"][side, end, k]
                total[ksel.start + k, pl.ds(row0, rows), :] = x

    swap = pltpu.make_async_remote_copy(
        src_ref=user_ref, dst_ref=user_out, send_sem=last.at[0], recv_sem=last.at[1], device_id=pair, device_id_type=MESH)
    done = set()
    swapped = False
    for key in TASK_ORDER:
        if key[0] == "pair":
            remote(key).start()
            continue
        if not swapped:
            swap.start()
            swapped = True
        for dep in sorted(TASKS[key]["deps"], key=lambda k: DONE_AT[k]):
            if dep[0] == "sum" or dep in done:
                continue
            if dep[0] == "pair":
                loads[dep[1]].wait()
            remote(dep).wait_recv()
            done.add(dep)
        work(key)
        if key[0] == "send":
            remote(key).start()
    keep = pltpu.make_async_copy(total, grad_out.at[:, pl.ds(row_mine, 64), :], last.at[2])
    give = pltpu.make_async_remote_copy(
        src_ref=total, dst_ref=grad_out.at[:, pl.ds(row_mine, 64), :], send_sem=last.at[3], recv_sem=last.at[4],
        device_id=pair, device_id_type=MESH)
    keep.start()
    give.start()
    for key in SEND_INDEX:
        if key not in done:
            if key[0] == "pair":
                loads[key[1]].wait()
            remote(key).wait_recv()
        remote(key).wait_send()
    swap.wait()
    keep.wait()
    give.wait()


def reduce_parts(slots, used, user_part):
    scratch = [pltpu.VMEM((8, 4, 4, 64, 256), jnp.bfloat16)] * 2
    for i in range(3):
        kk, rows, (na, nb, nc) = dims(i)
        unit = (kk, rows, 256)
        scratch += [pltpu.VMEM((nb, 2, nc // 2, na) + unit, jnp.bfloat16)] * 2
        scratch += [pltpu.VMEM((nb, na) + unit, jnp.float32)]
        scratch += [pltpu.VMEM((2, nb // 2, na) + unit, jnp.bfloat16)] * 2
        scratch += [pltpu.VMEM((na,) + unit, jnp.float32)]
        scratch += [pltpu.VMEM((2, na // 2) + unit, jnp.float32)] * 2
    count = len(SEND_INDEX)
    scratch += [
        pltpu.VMEM((2, 64, 256), jnp.float32),
        pltpu.SemaphoreType.DMA((count,)), pltpu.SemaphoreType.DMA((count,)),
        pltpu.SemaphoreType.DMA((8,)), pltpu.SemaphoreType.DMA((5,)),
    ]
    anywhere = pl.BlockSpec(memory_space=pl.ANY)
    return pl.pallas_call(
        reduce_kernel,
        out_shape=(
            jax.ShapeDtypeStruct(user_part.shape, jnp.float32),
            jax.ShapeDtypeStruct((2, 128, 256), jnp.float32),
        ),
        in_specs=[anywhere, pl.BlockSpec(memory_space=pltpu.SMEM), anywhere],
        out_specs=(anywhere, anywhere),
        scratch_shapes=scratch,
        name="reduce_parts",
        compiler_params=pltpu.CompilerParams(collective_id=1, has_side_effects=True, vmem_limit_bytes=56 * 2**20),
    )(slots.reshape(8, 4, 4, 128, 256), used, user_part)


GROUP, RING = 4, 16


def tiles_kernel(keys_ref, panels_ref, counts_ref, users_ref, slots_out, user_out, half, vbuf, cbuf, acc, stage, vsem, csem, ssem):
    tiles = counts_ref.shape[0]

    def key(i):
        return keys_ref[jnp.clip(i, 0, tiles - 1)]

    def owner(i):
        return lax.shift_right_logical(key(i), 11)

    def fetch(i):
        k = key(i)
        slot = lax.rem(i, RING)
        item = lax.shift_right_logical(k, 10)
        tile = lax.rem(lax.shift_right_logical(k, 3), 128)
        return (
            pltpu.make_async_copy(panels_ref.at[item], vbuf.at[slot], vsem.at[slot]),
            pltpu.make_async_copy(counts_ref.at[tile], cbuf.at[slot], csem.at[slot]),
        )

    def put(i):
        slot = lax.rem(i, RING)
        return pltpu.make_async_copy(stage.at[slot], slots_out.at[owner(i)], ssem.at[slot])

    def is_last(i):
        return (i == tiles - 1) | (owner(i) != owner(i + 1))

    def start(i, _):
        for c in fetch(i):
            c.start()
        return 0

    lax.fori_loop(0, RING, start, 0)
    half[...] = users_ref[...].astype(jnp.bfloat16)
    user_out[...] = jnp.zeros_like(user_out)
    acc[...] = jnp.zeros_like(acc)

    def group(g, _):
        base = g * GROUP
        for n in range(GROUP):
            i = base + n
            for c in fetch(i):
                c.wait()

            @pl.when((i >= RING) & is_last(i - RING))
            def _():
                put(i - RING).wait()

        errs = []
        for n in range(GROUP):
            i = base + n
            slot = lax.rem(i, RING)
            block = lax.rem(key(i), 8)
            u = half[block]
            v = vbuf[slot]
            predicted = lax.dot_general(u, v, (((1,), (1,)), ((), ())), preferred_element_type=jnp.float32)
            amount = cbuf[slot].astype(jnp.float32)
            weight = amount * (0.5 / 64.0) + 1.0 / 64.0
            errs.append((weight * (predicted - jnp.where(amount > 0, 1.0, 0.0))).astype(jnp.bfloat16))
        for n in range(GROUP):
            i = base + n
            slot = lax.rem(i, RING)
            block = lax.rem(key(i), 8)
            first = (i == 0) | (owner(i) != owner(i - 1))
            item_part = lax.dot_general(errs[n], half[block], (((0,), (0,)), ((), ())), preferred_element_type=jnp.float32)
            total = jnp.where(first, 0.0, acc[...]) + item_part
            acc[...] = total
            stage[slot] = total.astype(jnp.bfloat16)
            user_out[block] += jnp.dot(errs[n], vbuf[slot], preferred_element_type=jnp.float32)
        for n in range(GROUP):
            i = base + n

            @pl.when(is_last(i))
            def _():
                put(i).start()

            @pl.when(i + RING < tiles)
            def _():
                for c in fetch(i + RING):
                    c.start()

        return 0

    lax.fori_loop(0, tiles // GROUP, group, 0)

    def finish(n, _):
        i = tiles - RING + n

        @pl.when(is_last(i))
        def _():
            put(i).wait()

        return 0

    lax.fori_loop(0, RING, finish, 0)


def tile_parts(keys, panels, counts, users):
    anywhere = pl.BlockSpec(memory_space=pl.ANY)
    whole = pl.BlockSpec(memory_space=pltpu.VMEM)
    return pl.pallas_call(
        tiles_kernel,
        out_shape=(
            jax.ShapeDtypeStruct((128, 128, 256), jnp.bfloat16),
            jax.ShapeDtypeStruct((8, 128, 256), jnp.float32),
        ),
        in_specs=[pl.BlockSpec(memory_space=pltpu.SMEM), anywhere, anywhere, whole],
        out_specs=(anywhere, whole),
        scratch_shapes=[
            pltpu.VMEM((8, 128, 256), jnp.bfloat16),
            pltpu.VMEM((RING, 128, 256), jnp.bfloat16),
            pltpu.VMEM((RING, 128, 128), jnp.bfloat16),
            pltpu.VMEM((128, 256), jnp.float32),
            pltpu.VMEM((RING, 128, 256), jnp.bfloat16),
            pltpu.SemaphoreType.DMA((RING,)),
            pltpu.SemaphoreType.DMA((RING,)),
            pltpu.SemaphoreType.DMA((RING,)),
        ],
        name="tile_parts",
        compiler_params=pltpu.CompilerParams(vmem_limit_bytes=40 * 2**20),
        cost_estimate=pl.CostEstimate(flops=128 * 6 * 128 * 128 * 256, bytes_accessed=26 * 2**20, transcendentals=0),
    )(keys, panels, counts, users)


def sorted_keys(items, blocks):
    key = (items * 128 + jnp.arange(items.shape[0], dtype=jnp.int32)) * 8 + blocks
    rank = jnp.sum((key[None, :] < key[:, None]).astype(jnp.int32), axis=1)
    place = jnp.arange(items.shape[0], dtype=jnp.int32)
    return jnp.sum(jnp.where(rank[None, :] == place[:, None], key[None, :], 0), axis=1)


def adagrad(factors, accum, grad):
    new_accum = accum + grad * grad
    return factors - grad / jnp.sqrt(new_accum), new_accum


def local(user_factors, user_accum, item_factors, item_accum, tile_counts, tile_user, tile_item, send_list):
    counts = tile_counts[0, 0]
    items = tile_item[0, 0]
    keys = sorted_keys(items, tile_user[0, 0])
    panels, other_items = gather_panels(item_factors, items[None, :])
    both = jnp.stack([items, other_items[0]])
    used = jnp.any(both[:, :, None] == jnp.arange(256, dtype=jnp.int32), axis=1).astype(jnp.int32)
    slots, user_part = tile_parts(keys, panels.reshape(256, 128, 256), counts, user_factors.reshape(8, 128, 256))
    other_user, item_grad = reduce_parts(slots, used, user_part.reshape(1024, 256))
    user_grad = user_part.reshape(1024, 256) + other_user
    new_users, new_user_accum = adagrad(user_factors, user_accum, user_grad)
    new_items, new_item_accum = adagrad(item_factors, item_accum, item_grad.reshape(256, 256))
    return new_users, new_user_accum, new_items, new_item_accum


def solution(mesh):
    rows = P("users", None)
    return jax.shard_map(
        local,
        mesh=mesh,
        in_specs=(rows, rows, rows, rows, P("users", "rep", None, None, None), P("users", "rep", None), P("users", "rep", None), P("users", "rep", None)),
        out_specs=(rows, rows, rows, rows),
        check_vma=False,
    )
```

```python
import functools
import heapq

import jax
import jax.numpy as jnp
from jax import lax
from jax.experimental import pallas as pl
from jax.experimental.pallas import tpu as pltpu
from jax.sharding import PartitionSpec as P

MESH = pl.DeviceIdType.MESH
AXES = ("z", "x", "y")
SIZE = {"z": 8, "x": 4, "y": 4}
GATHER_STREAMS = (
    (slice(0, 2), 48, 16, ("x", "y", "z")),
    (slice(0, 1), 0, 48, ("y", "z", "x")),
    (slice(1, 2), 0, 48, ("x", "z", "y")),
)
RATE, PAIR_RATE, HOP, PAIR_HOP, ISSUE, AHEAD = 45e3, 500e3, 1.7, 0.8, 0.07, 2.5


def signed(j, n):
    return j if j <= n // 2 else j - n


def ring_steps(n):
    out = []
    for d in range(n // 2):
        for s in (1, -1):
            last = d == n // 2 - 1
            out.append((s, d, ((0,) if s == 1 else (1,)) if last else (0, 1)))
    return out


def gather_sends(streams):
    sends = {}
    for i, (panels, row0, rows, order) in enumerate(streams):
        a, b, c = order
        unit = (panels.stop - panels.start) * rows * 128 * 2
        na, nb, nc = SIZE[a], SIZE[b], SIZE[c]
        first = [(s, d, (0, 1)) for s, d, h in ring_steps(na) if s == 1 or d < na // 2 - 1]
        near = [(i, 1, 0, s, d) for s, d, h in first]

        def add(key, axis, h, deps, size, at):
            sends[key] = dict(axis=axis, s=key[3], h=h, deps=deps, size=size, at=at)

        for s, d, h in first:
            add((i, 1, 0, s, d), a, h, [] if d == 0 else [(i, 1, 0, s, d - 1)], unit * 2, {a: -s * d, b: 0, c: 0})
        for s, d, h in ring_steps(nb):
            deps = near if d == 0 else [(i, 2, 0, s, d - 1)]
            add((i, 2, 0, s, d), b, h, deps, unit * len(h) * na, {a: None, b: -s * d, c: 0})
        for j in range(nb):
            off = signed(j, nb)
            if off == 0:
                line = near
            elif off == nb // 2:
                line = [(i, 2, 0, s, nb // 2 - 1) for s in (1, -1)]
            else:
                line = [(i, 2, 0, -1 if off > 0 else 1, abs(off) - 1)]
            for s, d, h in ring_steps(nc):
                deps = line if d == 0 else [(i, 3, j, s, d - 1)]
                add((i, 3, j, s, d), c, h, deps, unit * len(h) * na, {a: None, b: off, c: -s * d})
            deps = line + [(i, 3, j, s, d) for s, d, h in ring_steps(nc)]
            add((i, 4, j, 0, 0), "pair", (0, 1), deps, unit * 2 * na * nc, {a: None, b: off, c: None})
    return sends


def timeline(sends, rank):
    users, waiting, ready, begin, arrive, queue, busy, events = {}, {}, {}, {}, {}, {}, {}, []
    core, count = 0.0, 0
    for k, v in sends.items():
        waiting[k] = len(v["deps"])
        for dep in v["deps"]:
            users.setdefault(dep, []).append(k)
        if not v["deps"]:
            ready[k] = 0.0
            heapq.heappush(events, (0.0, count, "ready", k))
            count += 1
    while events:
        now = events[0][0]
        touched = []
        while events and events[0][0] <= now + 1e-9:
            _, _, what, k = heapq.heappop(events)
            if what == "arrive":
                for q in users.get(k, ()):
                    waiting[q] -= 1
                    if waiting[q] == 0:
                        core = max(core, now) + ISSUE + sends[q].get("work", 0.0)
                        ready[q] = core
                        heapq.heappush(events, (core, count, "ready", q))
                        count += 1
            elif what == "ready":
                link = (sends[k]["axis"], sends[k]["s"])
                heapq.heappush(queue.setdefault(link, []), (rank(k), k))
                touched.append(link)
            else:
                touched.append(k)
        for link in touched:
            if queue.get(link) and busy.get(link, 0.0) <= now + 1e-6:
                _, k = heapq.heappop(queue[link])
                rate, delay = {"pair": (PAIR_RATE, PAIR_HOP), "core": (1e9, 0.0)}.get(link[0], (RATE, HOP))
                busy[link] = now + sends[k]["size"] / rate
                begin[k] = max(ready[k], now - AHEAD)
                arrive[k] = busy[link] + delay
                for when, what, item in ((busy[link], "free", link), (arrive[k], "arrive", k)):
                    heapq.heappush(events, (when, count, what, item))
                    count += 1
    return sorted(sends, key=lambda k: (begin[k], k)), arrive


def gather_plan(streams=GATHER_STREAMS):
    sends = gather_sends(streams)

    def rank(k):
        i, phase, j, s, d = k
        if phase == 4:
            return 0.0
        extra = (0, 6, 0)[i]
        if phase == 3:
            return 20 + extra - 0.5 * (SIZE[streams[i][3][2]] // 2 - d)
        return extra - d

    order, arrive = timeline(sends, rank)
    return streams, sends, order, arrive


def wrap(v, n):
    return lax.rem(v + 2 * n, n)


def coords():
    u = lax.axis_index("users")
    return {"z": u // 16, "x": lax.rem(u // 4, 4), "y": lax.rem(u, 4)}


def index_of(c):
    return c["z"] * 16 + c["x"] * 4 + c["y"]


def neighbour(me, axis, s):
    c = dict(me)
    c[axis] = wrap(me[axis] + s, SIZE[axis])
    return index_of(c)


def greet(me, rep):
    bar = pltpu.get_barrier_semaphore()
    for axis in AXES:
        for s in (1, -1):
            pl.semaphore_signal(bar, inc=1, device_id=(neighbour(me, axis, s), rep), device_id_type=MESH)
    pl.semaphore_signal(bar, inc=1, device_id=(index_of(me), 1 - rep), device_id_type=MESH)
    pl.semaphore_wait(bar, 7)


def gather_kernel(plan, own_ref, items_ref, out_ref, other_items_ref, raw, half, send, recv, local):
    streams, sends, order, arrive = plan
    index = {k: n for n, k in enumerate(order)}
    me = coords()
    rep = lax.axis_index("rep")
    bring = pltpu.make_async_copy(own_ref, raw, local.at[1])
    bring.start()
    greet(me, rep)
    bring.wait()
    half[...] = raw[...].reshape(2, 128, 256).astype(jnp.bfloat16)
    lines = pl.ds(pl.multiple_of(rep * 64, 64), 64)
    keep = pltpu.make_async_copy(half.at[:, lines], out_ref.at[me["z"], me["x"], me["y"], :, lines], local.at[0])
    keep.start()
    spot = {axis: {off: wrap(me[axis] + off, SIZE[axis]) for off in range(-(SIZE[axis] // 2), SIZE[axis] // 2 + 1)} for axis in AXES}
    close = {(axis, s): neighbour(me, axis, s) for axis in AXES for s in (1, -1)}
    pair = (index_of(me), 1 - rep)

    def copy(key):
        v = sends[key]
        panels, row0, rows, axes = streams[key[0]]
        where = []
        for axis in AXES:
            off = v["at"][axis]
            if off is not None:
                where.append(spot[axis][off])
            elif axis == axes[0] and len(v["h"]) == 1:
                where.append(pl.ds(SIZE[axis] // 2 * v["h"][0], SIZE[axis] // 2))
            else:
                where.append(slice(None))
        row = pl.ds(pl.multiple_of(rep * 64 + row0, 16), rows)
        place = tuple(where) + (panels, row)
        return pltpu.make_async_remote_copy(
            src_ref=half.at[panels, row] if not v["deps"] else out_ref.at[place],
            dst_ref=out_ref.at[place],
            send_sem=send.at[index[key]],
            recv_sem=recv.at[index[key]],
            device_id=pair if key[1] == 4 else (close[v["axis"], v["s"]], rep),
            device_id_type=MESH,
        )

    swap = pltpu.make_async_remote_copy(
        src_ref=items_ref, dst_ref=other_items_ref, send_sem=send.at[len(order)], recv_sem=recv.at[len(order)],
        device_id=pair, device_id_type=MESH,
    )
    done = set()
    kept = False
    for key in order:
        for dep in sorted(sends[key]["deps"], key=lambda k: arrive[k]):
            if dep not in done:
                copy(dep).wait_recv()
                done.add(dep)
        if sends[key]["deps"] and not kept:
            swap.start()
            keep.wait()
            kept = True
        copy(key).start()
    for key in sorted(order, key=lambda k: arrive[k]):
        if key not in done:
            copy(key).wait_recv()
    for key in order:
        copy(key).wait_send()
    swap.wait()


def gather_panels(own, items, plan=gather_plan(), cid=0, name="gather_panels"):
    count = len(plan[2]) + 1
    anywhere = pl.BlockSpec(memory_space=pl.ANY)
    return pl.pallas_call(
        functools.partial(gather_kernel, plan),
        out_shape=(
            jax.ShapeDtypeStruct((8, 4, 4, 2, 128, 256), jnp.bfloat16),
            jax.ShapeDtypeStruct(items.shape, items.dtype),
        ),
        in_specs=[anywhere, anywhere],
        out_specs=(anywhere, anywhere),
        scratch_shapes=[
            pltpu.VMEM((256, 256), jnp.float32),
            pltpu.VMEM((2, 128, 256), jnp.bfloat16),
            pltpu.SemaphoreType.DMA((count,)),
            pltpu.SemaphoreType.DMA((count,)),
            pltpu.SemaphoreType.DMA((2,)),
        ],
        name=name,
        compiler_params=pltpu.CompilerParams(collective_id=cid, has_side_effects=True, vmem_limit_bytes=56 * 2**20),
    )(own, items)


REDUCE_STREAMS = (
    (slice(0, 2), 48, 16, ("x", "y", "z")),
    (slice(0, 1), 0, 48, ("y", "z", "x")),
    (slice(1, 2), 0, 48, ("x", "z", "y")),
)


def reduce_steps(n):
    out = []
    for q in range(n // 2):
        for s in (1, -1):
            out.append((s, q, n // 2 - q, ((0,) if s == 1 else (1,)) if q == 0 else (0, 1)))
    return out


def far_first(n):
    out = [n // 2]
    for d in range(n // 2 - 1, 0, -1):
        out += [d, -d]
    return out + [0]


def reduce_plan():
    tasks = {}
    zs = far_first(8)
    for n, off in enumerate(zs):
        tasks[("pair", off)] = dict(kind="pair", deps=[], size=16 * 64 * 256 * 2, rank=n)
    allz = [("pair", off) for off in zs]
    for i, (ksel, row0, rows, order) in enumerate(REDUCE_STREAMS):
        a, b, c = order
        na, nb, nc = SIZE[a], SIZE[b], SIZE[c]
        unit = (ksel.stop - ksel.start) * rows * 128 * 2
        for rank, j in enumerate(far_first(nb)):
            def shares(dist_c):
                if b == "z":
                    return [("pair", j if j != -(nb // 2) else nb // 2)]
                if c == "z":
                    return [("pair", dist_c)]
                return allz
            for s, q, e, h in reduce_steps(nc):
                at = s * e
                if at == -(nc // 2):
                    at = nc // 2
                deps = shares(at) + ([("send", i, 1, j, s, q - 1)] if q else [])
                tasks[("send", i, 1, j, s, q)] = dict(kind="send", axis=c, s=s, h=h, deps=deps, size=unit * len(h) * na, rank=rank, e=s * e)
            last = nc // 2 - 1
            tasks[("sum", i, 1, j)] = dict(kind="sum", deps=shares(0) + [("send", i, 1, j, s, last) for s in (1, -1)], size=unit * 2 * na, rank=rank)
        for s, q, e, h in reduce_steps(nb):
            line = s * e if s * e != -(nb // 2) else nb // 2
            deps = [("sum", i, 1, line)] + ([("send", i, 2, 0, s, q - 1)] if q else [])
            tasks[("send", i, 2, 0, s, q)] = dict(kind="send", axis=b, s=s, h=h, deps=deps, size=unit * len(h) * na, rank=-5, e=line)
        tasks[("sum", i, 2)] = dict(kind="sum", deps=[("sum", i, 1, 0)] + [("send", i, 2, 0, s, nb // 2 - 1) for s in (1, -1)], size=unit * 2 * na, rank=-5)
        for s, q, e, h in reduce_steps(na):
            deps = [("sum", i, 2)] + ([("send", i, 3, 0, s, q - 1)] if q else [])
            tasks[("send", i, 3, 0, s, q)] = dict(kind="send", axis=a, s=s, h=h, deps=deps, size=2 * unit * len(h), rank=-9, e=s * e)
        tasks[("sum", i, 3)] = dict(kind="sum", deps=[("sum", i, 2)] + [("send", i, 3, 0, s, na // 2 - 1) for s in (1, -1)], size=unit * 2, rank=-9)
    for k, v in tasks.items():
        v["deps"] = list(dict.fromkeys(v["deps"]))
        if v["kind"] == "pair":
            v.update(axis="pair", s=0)
        else:
            v["work"] = v["size"] / WORK_RATE
            if v["kind"] == "sum":
                v.update(axis="core", s=k)
    pairs = [k for k in tasks if k[0] == "pair"]
    order, arrive = timeline(tasks, lambda k: reduce_rank(tasks[k], k))
    order = pairs + [k for k in order if k[0] != "pair"]
    placed, final = set(), []
    def place(k):
        if k not in placed:
            for dep in tasks[k]["deps"]:
                if dep[0] == "sum":
                    place(dep)
            placed.add(k)
            final.append(k)
    for k in order:
        place(k)
    return tasks, final, arrive


WORK_RATE = 600e3


def reduce_rank(v, k):
    if v["kind"] == "pair":
        return v["rank"]
    if v["kind"] == "sum":
        return 0.0
    return (5.0 + 4 * v["rank"], 10.0, 0.0)[k[2] - 1] - k[-1]


TASKS, TASK_ORDER, DONE_AT = reduce_plan()
SEND_INDEX = {k: n for n, k in enumerate([k for k in TASK_ORDER if k[0] != "sum"])}


def dims(i):
    ksel, row0, rows, order = REDUCE_STREAMS[i]
    return ksel.stop - ksel.start, rows, tuple(SIZE[x] for x in order)


def reduce_kernel(skip_work, skip_pair, slots_ref, used_ref, user_ref, user_out, grad_out, mine, other, *rest):
    bufs = [dict(zip(("s1", "r1", "l1", "s2", "r2", "l2", "s3", "r3"), rest[8 * i: 8 * i + 8])) for i in range(3)]
    total, send, recv, load, last = rest[24:]
    me = coords()
    rep = lax.axis_index("rep")
    row_mine = pl.multiple_of(rep * 64, 64)
    row_other = pl.multiple_of((1 - rep) * 64, 64)
    zof = {off: wrap(me["z"] + off, 8) for off in range(-4, 5)}
    loads = {}
    for n, off in enumerate(far_first(8)):
        loads[off] = pltpu.make_async_copy(slots_ref.at[zof[off], :, :, pl.ds(row_mine, 64), :], mine.at[zof[off]], load.at[n])
        loads[off].start()
    greet(me, rep)
    pair = (index_of(me), 1 - rep)

    def remote(key):
        if key[0] == "pair":
            z = zof[key[1]]
            return pltpu.make_async_remote_copy(
                src_ref=slots_ref.at[z, :, :, pl.ds(row_other, 64), :], dst_ref=other.at[z],
                send_sem=send.at[SEND_INDEX[key]], recv_sem=recv.at[SEND_INDEX[key]], device_id=pair, device_id_type=MESH)
        _, i, phase, j, s, q = key
        v = TASKS[key]
        nb = dims(i)[2][1]
        cols = pl.ds(0, 256) if len(v["h"]) == 2 else pl.ds(128 * v["h"][0], 128)
        side = 0 if s == 1 else 1
        at = (j % nb, side, q) if phase == 1 else (side, q)
        tail = (slice(None),) * (2 if phase == 3 else 3) + (cols,)
        return pltpu.make_async_remote_copy(
            src_ref=bufs[i]["s%d" % phase].at[at + tail], dst_ref=bufs[i]["r%d" % phase].at[at + tail],
            send_sem=send.at[SEND_INDEX[key]], recv_sem=recv.at[SEND_INDEX[key]],
            device_id=(neighbour(me, v["axis"], s), rep), device_id_type=MESH)

    def share(i, offs, n, cols):
        ksel, row0, rows, order = REDUCE_STREAMS[i]
        a, b, c = order
        where = {b: wrap(me[b] + offs[0], SIZE[b]), c: wrap(me[c] + offs[1], SIZE[c]), a: n}
        owner = index_of(where)
        place = (where["z"], where["x"], where["y"], pl.ds(row0, rows), cols)
        x = mine[place].astype(jnp.float32)
        y = other[place].astype(jnp.float32)
        out = []
        for k in range(ksel.start, ksel.stop):
            ux = used_ref[0, owner * 2 + k] > 0
            uy = used_ref[1, owner * 2 + k] > 0
            out.append(jnp.where(ux, x, 0.0) + jnp.where(uy, y, 0.0))
        return out

    def work(key):
        v = TASKS[key]
        i = key[1]
        kk, rows, (na, nb, nc) = dims(i)
        buf = bufs[i]
        if key[0] == "send":
            _, i, phase, j, s, q = key
            side = 0 if s == 1 else 1
            for h in ((0, 1) if (q == 1) else (None,)):
                cols = pl.ds(128 * h, 128) if h is not None else (pl.ds(0, 256) if len(v["h"]) == 2 else pl.ds(128 * v["h"][0], 128))
                got = q >= 2 or (q == 1 and h == side)

                def body(n, _, cols=cols, got=got):
                    if phase == 1:
                        parts = share(i, (j, v["e"]), n, cols)
                    elif phase == 2:
                        parts = [buf["l1"][v["e"] % nb, n, k, :, cols] for k in range(kk)]
                    for k in range(kk):
                        x = parts[k]
                        if phase == 1:
                            if got:
                                x = x + buf["r1"][j % nb, side, q - 1, n, k, :, cols].astype(jnp.float32)
                            buf["s1"][j % nb, side, q, n, k, :, cols] = x.astype(jnp.bfloat16)
                        else:
                            if got:
                                x = x + buf["r2"][side, q - 1, n, k, :, cols].astype(jnp.float32)
                            buf["s2"][side, q, n, k, :, cols] = x.astype(jnp.bfloat16)
                    return 0

                if phase == 3:
                    n = wrap(me[REDUCE_STREAMS[i][3][0]] + v["e"], na)
                    for k in range(kk):
                        x = buf["l2"][n, k, :, cols]
                        if got:
                            x = x + buf["r3"][side, q - 1, k, :, cols]
                        buf["s3"][side, q, k, :, cols] = x
                else:
                    lax.fori_loop(0, na, body, 0)
            return
        phase = key[2]
        end = {1: nc, 2: nb, 3: na}[phase] // 2 - 1
        full = pl.ds(0, 256)
        if phase == 1:
            j = key[3]

            def body(n, _):
                parts = share(i, (j, 0), n, full)
                for k in range(kk):
                    x = parts[k]
                    for side in range(2):
                        x = x + buf["r1"][j % nb, side, end, n, k].astype(jnp.float32)
                    buf["l1"][j % nb, n, k] = x
                return 0

            lax.fori_loop(0, na, body, 0)
        elif phase == 2:

            def body(n, _):
                for k in range(kk):
                    x = buf["l1"][0, n, k]
                    for side in range(2):
                        x = x + buf["r2"][side, end, n, k].astype(jnp.float32)
                    buf["l2"][n, k] = x
                return 0

            lax.fori_loop(0, na, body, 0)
        else:
            ksel, row0, rows, order = REDUCE_STREAMS[i]
            n = me[order[0]]
            for k in range(kk):
                x = buf["l2"][n, k]
                for side in range(2):
                    x = x + buf["r3"][side, end, k]
                total[ksel.start + k, pl.ds(row0, rows), :] = x

    swap = pltpu.make_async_remote_copy(
        src_ref=user_ref, dst_ref=user_out, send_sem=last.at[0], recv_sem=last.at[1], device_id=pair, device_id_type=MESH)
    done = set()
    swapped = False
    for key in TASK_ORDER:
        if key[0] == "pair":
            if not skip_pair:
                remote(key).start()
            continue
        if not swapped:
            swap.start()
            swapped = True
        for dep in sorted(TASKS[key]["deps"], key=lambda k: DONE_AT[k]):
            if dep[0] == "sum" or dep in done:
                continue
            if dep[0] == "pair":
                loads[dep[1]].wait()
                if skip_pair:
                    done.add(dep)
                    continue
            remote(dep).wait_recv()
            done.add(dep)
        if not skip_work:
            work(key)
        if key[0] == "send":
            remote(key).start()
    keep = pltpu.make_async_copy(total, grad_out.at[:, pl.ds(row_mine, 64), :], last.at[2])
    give = pltpu.make_async_remote_copy(
        src_ref=total, dst_ref=grad_out.at[:, pl.ds(row_mine, 64), :], send_sem=last.at[3], recv_sem=last.at[4],
        device_id=pair, device_id_type=MESH)
    keep.start()
    give.start()
    for key in SEND_INDEX:
        if skip_pair and key[0] == "pair":
            continue
        if key not in done:
            if key[0] == "pair":
                loads[key[1]].wait()
            remote(key).wait_recv()
        remote(key).wait_send()
    swap.wait()
    keep.wait()
    give.wait()


def reduce_parts(slots, used, user_part, skip_work=False, skip_pair=False, cid=1, name='reduce_parts'):
    scratch = [pltpu.VMEM((8, 4, 4, 64, 256), jnp.bfloat16)] * 2
    for i in range(3):
        kk, rows, (na, nb, nc) = dims(i)
        unit = (kk, rows, 256)
        scratch += [pltpu.VMEM((nb, 2, nc // 2, na) + unit, jnp.bfloat16)] * 2
        scratch += [pltpu.VMEM((nb, na) + unit, jnp.float32)]
        scratch += [pltpu.VMEM((2, nb // 2, na) + unit, jnp.bfloat16)] * 2
        scratch += [pltpu.VMEM((na,) + unit, jnp.float32)]
        scratch += [pltpu.VMEM((2, na // 2) + unit, jnp.float32)] * 2
    count = len(SEND_INDEX)
    scratch += [
        pltpu.VMEM((2, 64, 256), jnp.float32),
        pltpu.SemaphoreType.DMA((count,)), pltpu.SemaphoreType.DMA((count,)),
        pltpu.SemaphoreType.DMA((8,)), pltpu.SemaphoreType.DMA((5,)),
    ]
    anywhere = pl.BlockSpec(memory_space=pl.ANY)
    return pl.pallas_call(
        functools.partial(reduce_kernel, skip_work, skip_pair),
        out_shape=(
            jax.ShapeDtypeStruct(user_part.shape, jnp.float32),
            jax.ShapeDtypeStruct((2, 128, 256), jnp.float32),
        ),
        in_specs=[anywhere, pl.BlockSpec(memory_space=pltpu.SMEM), anywhere],
        out_specs=(anywhere, anywhere),
        scratch_shapes=scratch,
        name=name,
        compiler_params=pltpu.CompilerParams(collective_id=cid, has_side_effects=True, vmem_limit_bytes=56 * 2**20),
    )(slots.reshape(8, 4, 4, 128, 256), used, user_part)


GROUP, RING = 16, 32


def tiles_kernel(keys_ref, panels_ref, counts_ref, users_ref, slots_out, user_out, half, raw, usem, vbuf, cbuf, acc, stage, vsem, csem, ssem):
    tiles = counts_ref.shape[0]

    def key(i):
        return keys_ref[jnp.clip(i, 0, tiles - 1)]

    def owner(i):
        return lax.shift_right_logical(key(i), 11)

    def fetch(i):
        k = key(i)
        slot = lax.rem(i, RING)
        item = lax.shift_right_logical(k, 10)
        tile = lax.rem(lax.shift_right_logical(k, 3), 128)
        return (
            pltpu.make_async_copy(panels_ref.at[item], vbuf.at[slot], vsem.at[slot]),
            pltpu.make_async_copy(counts_ref.at[tile], cbuf.at[slot], csem.at[slot]),
        )

    def put(i):
        slot = lax.rem(i, RING)
        return pltpu.make_async_copy(stage.at[slot], slots_out.at[owner(i)], ssem.at[slot])

    def is_last(i):
        return (i == tiles - 1) | (owner(i) != owner(i + 1))

    def start(i, _):
        for c in fetch(i):
            c.start()
        return 0

    bring = pltpu.make_async_copy(users_ref, raw, usem)
    bring.start()
    lax.fori_loop(0, RING, start, 0)
    bring.wait()
    half[...] = raw[...].astype(jnp.bfloat16)
    user_out[...] = jnp.zeros_like(user_out)
    acc[...] = jnp.zeros_like(acc)

    def group(g, _):
        base = g * GROUP
        for n in range(GROUP):
            i = base + n
            for c in fetch(i):
                c.wait()

            @pl.when((i >= RING) & is_last(i - RING))
            def _():
                put(i - RING).wait()

        errs = []
        for n in range(GROUP):
            i = base + n
            slot = lax.rem(i, RING)
            block = lax.rem(key(i), 8)
            u = half[block]
            v = vbuf[slot]
            predicted = lax.dot_general(u, v, (((1,), (1,)), ((), ())), preferred_element_type=jnp.float32)
            amount = cbuf[slot].astype(jnp.float32)
            weight = amount * (0.5 / 64.0) + 1.0 / 64.0
            errs.append((weight * (predicted - jnp.where(amount > 0, 1.0, 0.0))).astype(jnp.bfloat16))
        for n in range(GROUP):
            i = base + n
            slot = lax.rem(i, RING)
            block = lax.rem(key(i), 8)
            first = (i == 0) | (owner(i) != owner(i - 1))
            item_part = lax.dot_general(errs[n], half[block], (((0,), (0,)), ((), ())), preferred_element_type=jnp.float32)
            total = jnp.where(first, 0.0, acc[...]) + item_part
            acc[...] = total
            stage[slot] = total.astype(jnp.bfloat16)
            user_out[block] += jnp.dot(errs[n], vbuf[slot], preferred_element_type=jnp.float32)
        for n in range(GROUP):
            i = base + n

            @pl.when(is_last(i))
            def _():
                put(i).start()

            @pl.when(i + RING < tiles)
            def _():
                for c in fetch(i + RING):
                    c.start()

        return 0

    lax.fori_loop(0, tiles // GROUP, group, 0)

    def finish(n, _):
        i = tiles - RING + n

        @pl.when(is_last(i))
        def _():
            put(i).wait()

        return 0

    lax.fori_loop(0, RING, finish, 0)


def tile_parts(keys, panels, counts, users):
    anywhere = pl.BlockSpec(memory_space=pl.ANY)
    whole = pl.BlockSpec(memory_space=pltpu.VMEM)
    return pl.pallas_call(
        tiles_kernel,
        out_shape=(
            jax.ShapeDtypeStruct((128, 128, 256), jnp.bfloat16),
            jax.ShapeDtypeStruct((8, 128, 256), jnp.float32),
        ),
        in_specs=[pl.BlockSpec(memory_space=pltpu.SMEM), anywhere, anywhere, anywhere],
        out_specs=(anywhere, whole),
        scratch_shapes=[
            pltpu.VMEM((8, 128, 256), jnp.bfloat16),
            pltpu.VMEM((8, 128, 256), jnp.float32),
            pltpu.SemaphoreType.DMA,
            pltpu.VMEM((RING, 128, 256), jnp.bfloat16),
            pltpu.VMEM((RING, 128, 128), jnp.bfloat16),
            pltpu.VMEM((128, 256), jnp.float32),
            pltpu.VMEM((RING, 128, 256), jnp.bfloat16),
            pltpu.SemaphoreType.DMA((RING,)),
            pltpu.SemaphoreType.DMA((RING,)),
            pltpu.SemaphoreType.DMA((RING,)),
        ],
        name="tile_parts",
        compiler_params=pltpu.CompilerParams(vmem_limit_bytes=58 * 2**20),
        cost_estimate=pl.CostEstimate(flops=128 * 6 * 128 * 128 * 256, bytes_accessed=26 * 2**20, transcendentals=0),
    )(keys, panels, counts, users)


def sorted_keys(items, blocks):
    key = (items * 128 + jnp.arange(items.shape[0], dtype=jnp.int32)) * 8 + blocks
    rank = jnp.sum((key[None, :] < key[:, None]).astype(jnp.int32), axis=1)
    place = jnp.arange(items.shape[0], dtype=jnp.int32)
    return jnp.sum(jnp.where(rank[None, :] == place[:, None], key[None, :], 0), axis=1)


def adagrad(factors, accum, grad):
    new_accum = accum + grad * grad
    return factors - grad / jnp.sqrt(new_accum), new_accum


def local(user_factors, user_accum, item_factors, item_accum, tile_counts, tile_user, tile_item, send_list):
    counts = tile_counts[0, 0]
    items = tile_item[0, 0]
    keys = sorted_keys(items, tile_user[0, 0])
    panels, other_items = gather_panels(item_factors, items[None, :])
    both = jnp.stack([items, other_items[0]])
    used = jnp.any(both[:, :, None] == jnp.arange(256, dtype=jnp.int32), axis=1).astype(jnp.int32)
    slots, user_part = tile_parts(keys, panels.reshape(256, 128, 256), counts, user_factors.reshape(8, 128, 256))
    other_user, item_grad = reduce_parts(slots, used, user_part.reshape(1024, 256))
    user_grad = user_part.reshape(1024, 256) + other_user
    new_users, new_user_accum = adagrad(user_factors, user_accum, user_grad)
    new_items, new_item_accum = adagrad(item_factors, item_accum, item_grad.reshape(256, 256))
    return new_users, new_user_accum, new_items, new_item_accum


def solution(mesh):
    rows = P("users", None)
    return jax.shard_map(
        local,
        mesh=mesh,
        in_specs=(rows, rows, rows, rows, P("users", "rep", None, None, None), P("users", "rep", None), P("users", "rep", None), P("users", "rep", None)),
        out_specs=(rows, rows, rows, rows),
        check_vma=False,
    )
```

```python
import functools
import heapq

import jax
import jax.numpy as jnp
from jax import lax
from jax.experimental import pallas as pl
from jax.experimental.pallas import tpu as pltpu
from jax.sharding import PartitionSpec as P

MESH = pl.DeviceIdType.MESH
AXES = ("z", "x", "y")
SIZE = {"z": 8, "x": 4, "y": 4}
GATHER_STREAMS = (
    (
        (slice(0, 2), 48, 16, ("x", "y", "z")),
        (slice(0, 1), 0, 48, ("y", "z", "x")),
        (slice(1, 2), 0, 48, ("x", "z", "y")),
    ),
    (
        (slice(1, 2), 48, 16, ("x", "y", "z")),
        (slice(0, 1), 0, 64, ("y", "z", "x")),
        (slice(1, 2), 0, 48, ("x", "z", "y")),
    ),
)
RATE, PAIR_RATE, HOP, PAIR_HOP, ISSUE, AHEAD = 43e3, 500e3, 1.7, 0.8, 0.07, 2.5


def signed(j, n):
    return j if j <= n // 2 else j - n


def ring_steps(n):
    out = []
    for d in range(n // 2):
        for s in (1, -1):
            last = d == n // 2 - 1
            out.append((s, d, ((0,) if s == 1 else (1,)) if last else (0, 1)))
    return out


def gather_sends(streams):
    sends = {}
    for i, (panels, row0, rows, order) in enumerate(streams):
        a, b, c = order
        unit = (panels.stop - panels.start) * rows * 128 * 2
        na, nb, nc = SIZE[a], SIZE[b], SIZE[c]
        first = [(s, d) for d in range(na // 2) for s in (1, -1) if (s == 1) == (i % 2 == 0) or d < na // 2 - 1]
        near = [(i, 1, 0, s, d) for s, d in first]

        def add(key, axis, h, deps, size, at):
            sends[key] = dict(axis=axis, s=key[3], h=h, deps=deps, size=size, at=at)

        for s, d in first:
            add((i, 1, 0, s, d), a, (0, 1), [], unit * 2, {a: 0, b: 0, c: 0})
            sends[i, 1, 0, s, d].update(hops=d + 1)
        for s, d, h in ring_steps(nb):
            deps = near if d == 0 else [(i, 2, 0, s, d - 1)]
            add((i, 2, 0, s, d), b, h, deps, unit * len(h) * na, {a: None, b: -s * d, c: 0})
        for j in range(nb):
            off = signed(j, nb)
            if off == 0:
                line = near
            elif off == nb // 2:
                line = [(i, 2, 0, s, nb // 2 - 1) for s in (1, -1)]
            else:
                line = [(i, 2, 0, -1 if off > 0 else 1, abs(off) - 1)]
            for s, d, h in ring_steps(nc):
                deps = line if d == 0 else [(i, 3, j, s, d - 1)]
                add((i, 3, j, s, d), c, h, deps, unit * len(h) * na, {a: None, b: off, c: -s * d})
            deps = line + [(i, 3, j, s, d) for s, d, h in ring_steps(nc)]
            add((i, 4, j, 0, 0), "pair", (0, 1), deps, unit * 2 * na * nc, {a: None, b: off, c: None})
    return sends


def timeline(sends, rank):
    users, waiting, ready, begin, arrive, queue, busy, events = {}, {}, {}, {}, {}, {}, {}, []
    core, count = 0.0, 0
    for k, v in sends.items():
        waiting[k] = len(v["deps"])
        for dep in v["deps"]:
            users.setdefault(dep, []).append(k)
        if not v["deps"]:
            ready[k] = 0.0
            heapq.heappush(events, (0.0, count, "ready", k))
            count += 1
    while events:
        now = events[0][0]
        touched = []
        while events and events[0][0] <= now + 1e-9:
            _, _, what, k = heapq.heappop(events)
            if what == "arrive":
                for q in users.get(k, ()):
                    waiting[q] -= 1
                    if waiting[q] == 0:
                        core = max(core, now) + ISSUE + sends[q].get("work", 0.0)
                        ready[q] = core
                        heapq.heappush(events, (core, count, "ready", q))
                        count += 1
            elif what == "ready":
                link = (sends[k]["axis"], sends[k]["s"])
                heapq.heappush(queue.setdefault(link, []), (rank(k), k))
                touched.append(link)
            else:
                touched.append(k)
        for link in touched:
            if queue.get(link) and busy.get(link, 0.0) <= now + 1e-6:
                _, k = heapq.heappop(queue[link])
                rate, delay = {"pair": (PAIR_RATE, PAIR_HOP), "core": (1e9, 0.0)}.get(link[0], (RATE, HOP))
                hops = sends[k].get("hops", 1)
                busy[link] = now + sends[k]["size"] * hops / rate
                begin[k] = max(ready[k], now - AHEAD)
                arrive[k] = busy[link] + delay + 0.4 * (hops - 1)
                for when, what, item in ((busy[link], "free", link), (arrive[k], "arrive", k)):
                    heapq.heappush(events, (when, count, what, item))
                    count += 1
    return sorted(sends, key=lambda k: (begin[k], k)), arrive


def gather_plan(streams):
    sends = gather_sends(streams)

    def rank(k):
        i, phase, j, s, d = k
        if phase == 4:
            return 0.0
        extra = (0, 0, 2)[i]
        if phase == 3:
            b, c = streams[i][3][1:]
            return 20 + extra - 2 * (SIZE[c] // 2 - d) + 0.3 * min(j, SIZE[b] - j)
        return extra - d

    order, arrive = timeline(sends, rank)
    return streams, sends, order, arrive


def wrap(v, n):
    return lax.rem(v + 2 * n, n)


def coords():
    u = lax.axis_index("users")
    return {"z": u // 16, "x": lax.rem(u // 4, 4), "y": lax.rem(u, 4)}


def index_of(c):
    return c["z"] * 16 + c["x"] * 4 + c["y"]


def neighbour(me, axis, s):
    c = dict(me)
    c[axis] = wrap(me[axis] + s, SIZE[axis])
    return index_of(c)


def greet(me, rep, far):
    bar = pltpu.get_barrier_semaphore()
    peers = [(axis, s) for axis in AXES for s in (1, -1)]
    peers += [(axis, s) for axis in far for s in range(2, SIZE[axis] - 1)]
    for axis, s in peers:
        pl.semaphore_signal(bar, inc=1, device_id=(neighbour(me, axis, s), rep), device_id_type=MESH)
    pl.semaphore_signal(bar, inc=1, device_id=(index_of(me), 1 - rep), device_id_type=MESH)
    pl.semaphore_wait(bar, len(peers) + 1)


def sort_keys(items, blocks):
    n = items.shape[-1]
    square = (n, n)
    key = (items * n + lax.broadcasted_iota(jnp.int32, (1, n), 1)) * 8 + blocks
    across = jnp.broadcast_to(key, square)
    down = jnp.transpose(across)
    rank = jnp.sum((down < across).astype(jnp.int32), axis=0, keepdims=True)
    rank_down = jnp.transpose(jnp.broadcast_to(rank, square))
    place = lax.broadcasted_iota(jnp.int32, square, 1)
    return jnp.sum(jnp.where(rank_down == place, down, 0), axis=0, keepdims=True)


def used_panels(items, count):
    down = jnp.transpose(jnp.broadcast_to(items, (items.shape[-1],) * 2))
    out = []
    for start in range(0, count, 128):
        panel = lax.broadcasted_iota(jnp.int32, down.shape, 1) + start
        out.append(jnp.max((down == panel).astype(jnp.int32), axis=0, keepdims=True))
    return jnp.concatenate(out, axis=1)


def gather_kernel(plans, own_ref, items_ref, blocks_ref, out_ref, keys_ref, used_ref, raw, half, other_items, send, recv, pair_recv, swap_sem, local):
    me = coords()
    rep = lax.axis_index("rep")
    bring = pltpu.make_async_copy(own_ref, raw, local.at[1])
    bring.start()
    greet(me, rep, sorted({stream[3][0] for streams, _, _, _ in plans for stream in streams}))
    bring.wait()
    half[...] = raw[...].reshape(2, 128, 256).astype(jnp.bfloat16)
    lines = pl.ds(pl.multiple_of(rep * 64, 64), 64)
    keep = pltpu.make_async_copy(half.at[:, lines], out_ref.at[me["z"], me["x"], me["y"], :, lines], local.at[0])
    keep.start()
    spot = {axis: {off: wrap(me[axis] + off, SIZE[axis]) for off in range(-(SIZE[axis] // 2), SIZE[axis] // 2 + 1)} for axis in AXES}
    close = {(axis, s): neighbour(me, axis, s) for axis in AXES for s in (1, -1)}
    pair = (index_of(me), 1 - rep)
    swap = pltpu.make_async_remote_copy(
        src_ref=items_ref, dst_ref=other_items, send_sem=swap_sem.at[0], recv_sem=swap_sem.at[1],
        device_id=pair, device_id_type=MESH,
    )

    def copy(side, key):
        streams, sends, order, arrive = plans[side]
        v = sends[key]
        panels, row0, rows, axes = streams[key[0]]
        where = []
        for axis in AXES:
            off = v["at"][axis]
            if off is not None:
                where.append(spot[axis][off])
            elif axis == axes[0] and len(v["h"]) == 1:
                where.append(pl.ds(SIZE[axis] // 2 * v["h"][0], SIZE[axis] // 2))
            else:
                where.append(slice(None))
        row = pl.ds(side * 64 + row0, rows)
        place = tuple(where) + (panels, row)
        number = order.index(key)
        arrival = recv.at[number]
        if key[1] == 4:
            target = pair
            arrival = pair_recv.at[side, number]
        elif key[1] == 1:
            target = (neighbour(me, v["axis"], v["s"] * (key[4] + 1)), rep)
        else:
            target = (close[v["axis"], v["s"]], rep)
        return pltpu.make_async_remote_copy(
            src_ref=half.at[panels, row] if not v["deps"] else out_ref.at[place],
            dst_ref=out_ref.at[place],
            send_sem=send.at[number],
            recv_sem=arrival,
            device_id=target,
            device_id_type=MESH,
        )

    def run(side):
        streams, sends, order, arrive = plans[side]
        done = set()
        kept = False
        for key in order:
            for dep in sorted(sends[key]["deps"], key=lambda k: arrive[k]):
                if dep not in done:
                    copy(side, dep).wait_recv()
                    done.add(dep)
            if sends[key]["deps"] and not kept:
                keep.wait()
                kept = True
            copy(side, key).start()
            if key[1] == 3 and "swap" not in done:
                done.add("swap")
                swap.start()
                keys_ref[...] = sort_keys(items_ref[...], blocks_ref[...])
                used_ref[0:1, :] = used_panels(items_ref[...], used_ref.shape[1])
        for key in sorted(order, key=lambda k: arrive[k]):
            if key[1] != 4 and key not in done:
                copy(side, key).wait_recv()
        swap.wait()
        used_ref[1:2, :] = used_panels(other_items[...], used_ref.shape[1])
        for key in plans[1 - side][2]:
            if key[1] == 4:
                copy(1 - side, key).wait_recv()
        for key in order:
            copy(side, key).wait_send()

    for side in range(2):
        pl.when(rep == side)(functools.partial(run, side))


def gather_panels(own, items, blocks, cid=0, name="gather_panels"):
    plans = tuple(gather_plan(streams) for streams in GATHER_STREAMS)
    count = max(len(plan[2]) for plan in plans)
    anywhere = pl.BlockSpec(memory_space=pl.ANY)
    whole = pl.BlockSpec(memory_space=pltpu.VMEM)
    return pl.pallas_call(
        functools.partial(gather_kernel, plans),
        out_shape=(
            jax.ShapeDtypeStruct((8, 4, 4, 2, 128, 256), jnp.bfloat16),
            jax.ShapeDtypeStruct(items.shape, jnp.int32),
            jax.ShapeDtypeStruct((2, 256), jnp.int32),
        ),
        in_specs=[anywhere, whole, whole],
        out_specs=(anywhere, whole, whole),
        scratch_shapes=[
            pltpu.VMEM((256, 256), jnp.float32),
            pltpu.VMEM((2, 128, 256), jnp.bfloat16),
            pltpu.VMEM(items.shape, jnp.int32),
            pltpu.SemaphoreType.DMA((count,)),
            pltpu.SemaphoreType.DMA((count,)),
            pltpu.SemaphoreType.DMA((2, count)),
            pltpu.SemaphoreType.DMA((2,)),
            pltpu.SemaphoreType.DMA((2,)),
        ],
        name=name,
        compiler_params=pltpu.CompilerParams(collective_id=cid, has_side_effects=True, vmem_limit_bytes=56 * 2**20),
    )(own, items, blocks)


REDUCE_STREAMS = (
    (slice(0, 2), 48, 16, ("y", "x", "z")),
    (slice(0, 1), 0, 48, ("y", "z", "x")),
    (slice(1, 2), 0, 48, ("x", "z", "y")),
)


def reduce_steps(n):
    out = []
    for q in range(n // 2):
        for s in (1, -1):
            out.append((s, q, n // 2 - q, ((0,) if s == 1 else (1,)) if q == 0 else (0, 1)))
    return out


def direct(i, n):
    return [(s, q, s * (q + 1)) for q in range(n // 2) for s in (1, -1) if (s == 1) == (i % 2 == 0) or q < n // 2 - 1]


def far_first(n):
    out = [n // 2]
    for d in range(n // 2 - 1, 0, -1):
        out += [d, -d]
    return out + [0]


def reduce_plan():
    tasks = {}
    zs = far_first(8)
    for n, off in enumerate(zs):
        tasks[("pair", off)] = dict(kind="pair", deps=[], size=16 * 64 * 256 * 2, rank=n)
    allz = [("pair", off) for off in zs]
    for i, (ksel, row0, rows, order) in enumerate(REDUCE_STREAMS):
        a, b, c = order
        na, nb, nc = SIZE[a], SIZE[b], SIZE[c]
        unit = (ksel.stop - ksel.start) * rows * 128 * 2
        for rank, j in enumerate(far_first(nb)):
            def shares(dist_c):
                if b == "z":
                    return [("pair", j if j != -(nb // 2) else nb // 2)]
                if c == "z":
                    return [("pair", dist_c)]
                return allz
            for s, q, e, h in reduce_steps(nc):
                at = s * e
                if at == -(nc // 2):
                    at = nc // 2
                deps = shares(at) + ([("send", i, 1, j, s, q - 1)] if q else [])
                tasks[("send", i, 1, j, s, q)] = dict(kind="send", axis=c, s=s, h=h, deps=deps, size=unit * len(h) * na, rank=rank, e=s * e)
            last = nc // 2 - 1
            tasks[("sum", i, 1, j)] = dict(kind="sum", deps=shares(0) + [("send", i, 1, j, s, last) for s in (1, -1)], size=unit * 2 * na, rank=rank)
        for s, q, e, h in reduce_steps(nb):
            line = s * e if s * e != -(nb // 2) else nb // 2
            deps = [("sum", i, 1, line)] + ([("send", i, 2, 0, s, q - 1)] if q else [])
            tasks[("send", i, 2, 0, s, q)] = dict(kind="send", axis=b, s=s, h=h, deps=deps, size=unit * len(h) * na, rank=-5, e=line)
        tasks[("sum", i, 2)] = dict(kind="sum", deps=[("sum", i, 1, 0)] + [("send", i, 2, 0, s, nb // 2 - 1) for s in (1, -1)], size=unit * 2 * na, rank=-5)
        for s, q, e in direct(i, na):
            tasks[("send", i, 3, 0, s, q)] = dict(kind="send", axis=a, s=s, h=(0, 1), deps=[("sum", i, 2)], size=4 * unit, rank=-9, e=e, hops=q + 1)
        tasks[("sum", i, 3)] = dict(kind="sum", deps=[("sum", i, 2)] + [("send", i, 3, 0, s, q) for s, q, e in direct(i, na)], size=unit * 2, rank=-9)
    for k, v in tasks.items():
        v["deps"] = list(dict.fromkeys(v["deps"]))
        if v["kind"] == "pair":
            v.update(axis="pair", s=0)
        else:
            v["work"] = v["size"] / WORK_RATE
            if v["kind"] == "sum":
                v.update(axis="core", s=k)
    pairs = [k for k in tasks if k[0] == "pair"]
    order, arrive = timeline(tasks, lambda k: reduce_rank(tasks[k], k))
    order = pairs + [k for k in order if k[0] != "pair"]
    placed, final = set(), []
    def place(k):
        if k not in placed:
            for dep in tasks[k]["deps"]:
                if dep[0] == "sum":
                    place(dep)
            placed.add(k)
            final.append(k)
    for k in order:
        place(k)
    return tasks, final, arrive


WORK_RATE = 600e3


def reduce_rank(v, k):
    if v["kind"] == "pair":
        return v["rank"]
    if v["kind"] == "sum":
        return 0.0
    return (10.0 + v["rank"], 0.0, 0.0)[k[2] - 1] + (0.0, 12.0, 12.0)[k[1]]


TASKS, TASK_ORDER, DONE_AT = reduce_plan()
SEND_INDEX = {k: n for n, k in enumerate([k for k in TASK_ORDER if k[0] != "sum"])}


def dims(i):
    ksel, row0, rows, order = REDUCE_STREAMS[i]
    return ksel.stop - ksel.start, rows, tuple(SIZE[x] for x in order)


def reduce_kernel(slots_ref, used_ref, user_ref, user_out, grad_out, mine, other, *rest):
    bufs = [dict(zip(("s1", "r1", "l1", "s2", "r2", "l2", "s3", "r3"), rest[8 * i: 8 * i + 8])) for i in range(3)]
    total, send, recv, load, last = rest[24:]
    me = coords()
    rep = lax.axis_index("rep")
    row_mine = pl.multiple_of(rep * 64, 64)
    row_other = pl.multiple_of((1 - rep) * 64, 64)
    zof = {off: wrap(me["z"] + off, 8) for off in range(-4, 5)}
    loads = {}
    for n, off in enumerate(far_first(8)):
        loads[off] = pltpu.make_async_copy(slots_ref.at[zof[off], :, :, pl.ds(row_mine, 64), :], mine.at[zof[off]], load.at[n])
        loads[off].start()
    greet(me, rep, sorted({stream[3][0] for stream in REDUCE_STREAMS}))
    pair = (index_of(me), 1 - rep)

    def remote(key):
        if key[0] == "pair":
            z = zof[key[1]]
            return pltpu.make_async_remote_copy(
                src_ref=slots_ref.at[z, :, :, pl.ds(row_other, 64), :], dst_ref=other.at[z],
                send_sem=send.at[SEND_INDEX[key]], recv_sem=recv.at[SEND_INDEX[key]], device_id=pair, device_id_type=MESH)
        _, i, phase, j, s, q = key
        v = TASKS[key]
        nb = dims(i)[2][1]
        cols = pl.ds(0, 256) if len(v["h"]) == 2 else pl.ds(128 * v["h"][0], 128)
        side = 0 if s == 1 else 1
        at = (j % nb, side, q) if phase == 1 else (side, q)
        tail = (slice(None),) * (2 if phase == 3 else 3) + (cols,)
        return pltpu.make_async_remote_copy(
            src_ref=bufs[i]["s%d" % phase].at[at + tail], dst_ref=bufs[i]["r%d" % phase].at[at + tail],
            send_sem=send.at[SEND_INDEX[key]], recv_sem=recv.at[SEND_INDEX[key]],
            device_id=(neighbour(me, v["axis"], v["e"] if phase == 3 else s), rep), device_id_type=MESH)

    def share(i, offs, n, cols):
        ksel, row0, rows, order = REDUCE_STREAMS[i]
        a, b, c = order
        where = {b: wrap(me[b] + offs[0], SIZE[b]), c: wrap(me[c] + offs[1], SIZE[c]), a: n}
        owner = index_of(where)
        place = (where["z"], where["x"], where["y"], pl.ds(row0, rows), cols)
        x = mine[place].astype(jnp.float32)
        y = other[place].astype(jnp.float32)
        out = []
        for k in range(ksel.start, ksel.stop):
            ux = used_ref[0, owner * 2 + k] > 0
            uy = used_ref[1, owner * 2 + k] > 0
            out.append(jnp.where(ux, x, 0.0) + jnp.where(uy, y, 0.0))
        return out

    def work(key):
        v = TASKS[key]
        i = key[1]
        kk, rows, (na, nb, nc) = dims(i)
        buf = bufs[i]
        if key[0] == "send":
            _, i, phase, j, s, q = key
            side = 0 if s == 1 else 1
            if phase == 3:
                n = wrap(me[REDUCE_STREAMS[i][3][0]] + v["e"], na)
                buf["s3"][side, q] = buf["l2"][n]
                return
            for h in ((0, 1) if (q == 1) else (None,)):
                cols = pl.ds(128 * h, 128) if h is not None else (pl.ds(0, 256) if len(v["h"]) == 2 else pl.ds(128 * v["h"][0], 128))
                got = q >= 2 or (q == 1 and h == side)

                def body(n, _, cols=cols, got=got):
                    if phase == 1:
                        parts = share(i, (j, v["e"]), n, cols)
                    elif phase == 2:
                        parts = [buf["l1"][v["e"] % nb, n, k, :, cols] for k in range(kk)]
                    for k in range(kk):
                        x = parts[k]
                        if phase == 1:
                            if got:
                                x = x + buf["r1"][j % nb, side, q - 1, n, k, :, cols].astype(jnp.float32)
                            buf["s1"][j % nb, side, q, n, k, :, cols] = x.astype(jnp.bfloat16)
                        else:
                            if got:
                                x = x + buf["r2"][side, q - 1, n, k, :, cols].astype(jnp.float32)
                            buf["s2"][side, q, n, k, :, cols] = x.astype(jnp.bfloat16)
                    return 0

                lax.fori_loop(0, na, body, 0)
            return
        phase = key[2]
        end = {1: nc, 2: nb, 3: na}[phase] // 2 - 1
        full = pl.ds(0, 256)
        if phase == 1:
            j = key[3]

            def body(n, _):
                parts = share(i, (j, 0), n, full)
                for k in range(kk):
                    x = parts[k]
                    for side in range(2):
                        x = x + buf["r1"][j % nb, side, end, n, k].astype(jnp.float32)
                    buf["l1"][j % nb, n, k] = x
                return 0

            lax.fori_loop(0, na, body, 0)
        elif phase == 2:

            def body(n, _):
                for k in range(kk):
                    x = buf["l1"][0, n, k]
                    for side in range(2):
                        x = x + buf["r2"][side, end, n, k].astype(jnp.float32)
                    buf["l2"][n, k] = x
                return 0

            lax.fori_loop(0, na, body, 0)
        else:
            ksel, row0, rows, order = REDUCE_STREAMS[i]
            n = me[order[0]]
            for k in range(kk):
                x = buf["l2"][n, k]
                for s, q, e in direct(i, na):
                    x = x + buf["r3"][0 if s == 1 else 1, q, k]
                total[ksel.start + k, pl.ds(row0, rows), :] = x

    swap = pltpu.make_async_remote_copy(
        src_ref=user_ref, dst_ref=user_out, send_sem=last.at[0], recv_sem=last.at[1], device_id=pair, device_id_type=MESH)
    done = set()
    swapped = False
    for key in TASK_ORDER:
        if key[0] == "pair":
            remote(key).start()
            continue
        if not swapped:
            swap.start()
            swapped = True
        for dep in sorted(TASKS[key]["deps"], key=lambda k: DONE_AT[k]):
            if dep[0] == "sum" or dep in done:
                continue
            if dep[0] == "pair":
                loads[dep[1]].wait()
            remote(dep).wait_recv()
            done.add(dep)
        work(key)
        if key[0] == "send":
            remote(key).start()
    keep = pltpu.make_async_copy(total, grad_out.at[:, pl.ds(row_mine, 64), :], last.at[2])
    give = pltpu.make_async_remote_copy(
        src_ref=total, dst_ref=grad_out.at[:, pl.ds(row_mine, 64), :], send_sem=last.at[3], recv_sem=last.at[4],
        device_id=pair, device_id_type=MESH)
    keep.start()
    give.start()
    for key in SEND_INDEX:
        if key not in done:
            if key[0] == "pair":
                loads[key[1]].wait()
            remote(key).wait_recv()
        remote(key).wait_send()
    swap.wait()
    keep.wait()
    give.wait()


def reduce_parts(slots, used, user_part, cid=1, name='reduce_parts'):
    scratch = [pltpu.VMEM((8, 4, 4, 64, 256), jnp.bfloat16)] * 2
    for i in range(3):
        kk, rows, (na, nb, nc) = dims(i)
        unit = (kk, rows, 256)
        scratch += [pltpu.VMEM((nb, 2, nc // 2, na) + unit, jnp.bfloat16)] * 2
        scratch += [pltpu.VMEM((nb, na) + unit, jnp.float32)]
        scratch += [pltpu.VMEM((2, nb // 2, na) + unit, jnp.bfloat16)] * 2
        scratch += [pltpu.VMEM((na,) + unit, jnp.float32)]
        scratch += [pltpu.VMEM((2, na // 2) + unit, jnp.float32)] * 2
    count = len(SEND_INDEX)
    scratch += [
        pltpu.VMEM((2, 64, 256), jnp.float32),
        pltpu.SemaphoreType.DMA((count,)), pltpu.SemaphoreType.DMA((count,)),
        pltpu.SemaphoreType.DMA((8,)), pltpu.SemaphoreType.DMA((5,)),
    ]
    anywhere = pl.BlockSpec(memory_space=pl.ANY)
    return pl.pallas_call(
        reduce_kernel,
        out_shape=(
            jax.ShapeDtypeStruct(user_part.shape, jnp.float32),
            jax.ShapeDtypeStruct((2, 128, 256), jnp.float32),
        ),
        in_specs=[anywhere, pl.BlockSpec(memory_space=pltpu.SMEM), anywhere],
        out_specs=(anywhere, anywhere),
        scratch_shapes=scratch,
        name=name,
        compiler_params=pltpu.CompilerParams(collective_id=cid, has_side_effects=True, vmem_limit_bytes=56 * 2**20),
    )(slots.reshape(8, 4, 4, 128, 256), used, user_part)


GROUP, RING = 16, 32


def tiles_kernel(keys_ref, panels_ref, counts_ref, users_ref, slots_out, user_out, half, raw, usem, vbuf, cbuf, acc, stage, vsem, csem, ssem):
    tiles = counts_ref.shape[0]

    def key(i):
        return keys_ref[jnp.clip(i, 0, tiles - 1)]

    def owner(i):
        return lax.shift_right_logical(key(i), 11)

    def fetch(i):
        k = key(i)
        slot = lax.rem(i, RING)
        item = lax.shift_right_logical(k, 10)
        tile = lax.rem(lax.shift_right_logical(k, 3), 128)
        return (
            pltpu.make_async_copy(panels_ref.at[item], vbuf.at[slot], vsem.at[slot]),
            pltpu.make_async_copy(counts_ref.at[tile], cbuf.at[slot], csem.at[slot]),
        )

    def put(i):
        slot = lax.rem(i, RING)
        return pltpu.make_async_copy(stage.at[slot], slots_out.at[owner(i)], ssem.at[slot])

    def is_last(i):
        return (i == tiles - 1) | (owner(i) != owner(i + 1))

    def start(i, _):
        for c in fetch(i):
            c.start()
        return 0

    bring = pltpu.make_async_copy(users_ref, raw, usem)
    bring.start()
    lax.fori_loop(0, RING, start, 0)
    bring.wait()
    half[...] = raw[...].astype(jnp.bfloat16)
    user_out[...] = jnp.zeros_like(user_out)
    acc[...] = jnp.zeros_like(acc)

    def group(g, _):
        base = g * GROUP
        for n in range(GROUP):
            i = base + n
            for c in fetch(i):
                c.wait()

            @pl.when((i >= RING) & is_last(i - RING))
            def _():
                put(i - RING).wait()

        errs = []
        for n in range(GROUP):
            i = base + n
            slot = lax.rem(i, RING)
            block = lax.rem(key(i), 8)
            u = half[block]
            v = vbuf[slot]
            predicted = lax.dot_general(u, v, (((1,), (1,)), ((), ())), preferred_element_type=jnp.float32)
            amount = cbuf[slot].astype(jnp.float32)
            weight = amount * (0.5 / 64.0) + 1.0 / 64.0
            errs.append((weight * (predicted - jnp.where(amount > 0, 1.0, 0.0))).astype(jnp.bfloat16))
        for n in range(GROUP):
            i = base + n
            slot = lax.rem(i, RING)
            block = lax.rem(key(i), 8)
            first = (i == 0) | (owner(i) != owner(i - 1))
            item_part = lax.dot_general(errs[n], half[block], (((0,), (0,)), ((), ())), preferred_element_type=jnp.float32)
            total = jnp.where(first, 0.0, acc[...]) + item_part
            acc[...] = total
            stage[slot] = total.astype(jnp.bfloat16)
            user_out[block] += jnp.dot(errs[n], vbuf[slot], preferred_element_type=jnp.float32)
        for n in range(GROUP):
            i = base + n

            @pl.when(is_last(i))
            def _():
                put(i).start()

            @pl.when(i + RING < tiles)
            def _():
                for c in fetch(i + RING):
                    c.start()

        return 0

    lax.fori_loop(0, tiles // GROUP, group, 0)

    def finish(n, _):
        i = tiles - RING + n

        @pl.when(is_last(i))
        def _():
            put(i).wait()

        return 0

    lax.fori_loop(0, RING, finish, 0)


def tile_parts(keys, panels, counts, users):
    anywhere = pl.BlockSpec(memory_space=pl.ANY)
    whole = pl.BlockSpec(memory_space=pltpu.VMEM)
    return pl.pallas_call(
        tiles_kernel,
        out_shape=(
            jax.ShapeDtypeStruct((128, 128, 256), jnp.bfloat16),
            jax.ShapeDtypeStruct((8, 128, 256), jnp.float32),
        ),
        in_specs=[pl.BlockSpec(memory_space=pltpu.SMEM), anywhere, anywhere, anywhere],
        out_specs=(anywhere, whole),
        scratch_shapes=[
            pltpu.VMEM((8, 128, 256), jnp.bfloat16),
            pltpu.VMEM((8, 128, 256), jnp.float32),
            pltpu.SemaphoreType.DMA,
            pltpu.VMEM((RING, 128, 256), jnp.bfloat16),
            pltpu.VMEM((RING, 128, 128), jnp.bfloat16),
            pltpu.VMEM((128, 256), jnp.float32),
            pltpu.VMEM((RING, 128, 256), jnp.bfloat16),
            pltpu.SemaphoreType.DMA((RING,)),
            pltpu.SemaphoreType.DMA((RING,)),
            pltpu.SemaphoreType.DMA((RING,)),
        ],
        name="tile_parts",
        compiler_params=pltpu.CompilerParams(vmem_limit_bytes=58 * 2**20),
        cost_estimate=pl.CostEstimate(flops=128 * 6 * 128 * 128 * 256, bytes_accessed=26 * 2**20, transcendentals=0),
    )(keys, panels, counts, users)


def adagrad_kernel(part, other, users, user_accum, grad, items, item_accum, new_users, new_user_accum, new_items, new_item_accum):
    for g, factors, accum, new, new_accum in (
        (part[...] + other[...], users, user_accum, new_users, new_user_accum),
        (grad[...], items, item_accum, new_items, new_item_accum),
    ):
        total = accum[...] + g * g
        new_accum[...] = total
        new[...] = factors[...] - g / jnp.sqrt(total)


def adagrad(part, other, users, user_accum, grad, items, item_accum, steps=4):
    def rows(x):
        return pl.BlockSpec((x.shape[0] // steps, x.shape[1]), lambda n: (n, 0))

    args = (part, other, users, user_accum, grad, items, item_accum)
    outs = (users, user_accum, items, item_accum)
    return pl.pallas_call(
        adagrad_kernel,
        grid=(steps,),
        out_shape=tuple(jax.ShapeDtypeStruct(x.shape, x.dtype) for x in outs),
        in_specs=[rows(x) for x in args],
        out_specs=tuple(rows(x) for x in outs),
        name="adagrad",
        compiler_params=pltpu.CompilerParams(vmem_limit_bytes=56 * 2**20),
    )(*args)


def local(user_factors, user_accum, item_factors, item_accum, tile_counts, tile_user, tile_item, send_list):
    counts = tile_counts[0, 0]
    panels, keys, used = gather_panels(item_factors, tile_item[0], tile_user[0])
    slots, user_part = tile_parts(keys[0], panels.reshape(256, 128, 256), counts, user_factors.reshape(8, 128, 256))
    other_user, item_grad = reduce_parts(slots, used, user_part.reshape(1024, 256))
    return adagrad(
        user_part.reshape(1024, 256), other_user, user_factors, user_accum,
        item_grad.reshape(256, 256), item_factors, item_accum,
    )


def solution(mesh):
    rows = P("users", None)
    return jax.shard_map(
        local,
        mesh=mesh,
        in_specs=(rows, rows, rows, rows, P("users", "rep", None, None, None), P("users", "rep", None), P("users", "rep", None), P("users", "rep", None)),
        out_specs=(rows, rows, rows, rows),
        check_vma=False,
    )
```

```python
import functools
import heapq

import jax
import jax.numpy as jnp
from jax import lax
from jax.experimental import pallas as pl
from jax.experimental.pallas import tpu as pltpu
from jax.sharding import PartitionSpec as P

MESH = pl.DeviceIdType.MESH
AXES = ("z", "x", "y")
SIZE = {"z": 8, "x": 4, "y": 4}
GATHER_STREAMS = (
    (
        (slice(0, 2), 48, 16, ("x", "y", "z")),
        (slice(0, 1), 0, 48, ("y", "z", "x")),
        (slice(1, 2), 0, 48, ("x", "z", "y")),
    ),
    (
        (slice(1, 2), 48, 16, ("x", "y", "z")),
        (slice(0, 1), 0, 64, ("y", "z", "x")),
        (slice(1, 2), 0, 48, ("x", "z", "y")),
    ),
)
PAIR_LOAD = 5 / 3
RATE, PAIR_RATE, HOP, PAIR_HOP, ISSUE, AHEAD = 43e3, 500e3, 1.7, 0.8, 0.07, 2.5


def signed(j, n):
    return j if j <= n // 2 else j - n


def ring_steps(n):
    out = []
    for d in range(n // 2):
        for s in (1, -1):
            last = d == n // 2 - 1
            out.append((s, d, ((0,) if s == 1 else (1,)) if last else (0, 1)))
    return out


def gather_sends(streams):
    sends = {}
    for i, (panels, row0, rows, order) in enumerate(streams):
        a, b, c = order
        unit = (panels.stop - panels.start) * rows * 128 * 2
        na, nb, nc = SIZE[a], SIZE[b], SIZE[c]
        first = [(s, d) for d in range(na // 2) for s in (1, -1) if (s == 1) == (i % 2 == 0) or d < na // 2 - 1]
        near = [(i, 1, 0, s, d) for s, d in first]

        def add(key, axis, h, deps, size, at):
            sends[key] = dict(axis=axis, s=key[3], h=h, deps=deps, size=size, at=at)

        for s, d in first:
            add((i, 1, 0, s, d), a, (0, 1), [], unit * 2, {a: 0, b: 0, c: 0})
            sends[i, 1, 0, s, d].update(hops=d + 1)
        for s, d, h in ring_steps(nb):
            deps = near if d == 0 else [(i, 2, 0, s, d - 1)]
            add((i, 2, 0, s, d), b, h, deps, unit * len(h) * na, {a: None, b: -s * d, c: 0})
        for j in range(nb):
            off = signed(j, nb)
            if off == 0:
                line = near
            elif off == nb // 2:
                line = [(i, 2, 0, s, nb // 2 - 1) for s in (1, -1)]
            else:
                line = [(i, 2, 0, -1 if off > 0 else 1, abs(off) - 1)]
            for s, d, h in ring_steps(nc):
                deps = line if d == 0 else [(i, 3, j, s, d - 1)]
                add((i, 3, j, s, d), c, h, deps, unit * len(h) * na, {a: None, b: off, c: -s * d})
            if abs(off) < nb // 2:
                deps = line + [(i, 3, j, s, d) for s, d, h in ring_steps(nc)]
                add((i, 4, j, 0, 0), "pair", (0, 1), deps, unit * 2 * na * nc * PAIR_LOAD, {a: None, b: off, c: None})
                continue
            for m in range(nc):
                far = signed(m, nc)
                if far == 0:
                    deps = line
                elif far == nc // 2:
                    deps = [(i, 3, j, s, nc // 2 - 1) for s in (1, -1)]
                else:
                    deps = [(i, 3, j, -1 if far > 0 else 1, abs(far) - 1)]
                add((i, 4, j, 0, m), "pair", (0, 1), deps, unit * 2 * na * PAIR_LOAD, {a: None, b: off, c: far})
    return sends


def timeline(sends, rank):
    users, waiting, ready, begin, arrive, queue, busy, events = {}, {}, {}, {}, {}, {}, {}, []
    core, count = 0.0, 0
    for k, v in sends.items():
        waiting[k] = len(v["deps"])
        for dep in v["deps"]:
            users.setdefault(dep, []).append(k)
        if not v["deps"]:
            ready[k] = 0.0
            heapq.heappush(events, (0.0, count, "ready", k))
            count += 1
    while events:
        now = events[0][0]
        touched = []
        while events and events[0][0] <= now + 1e-9:
            _, _, what, k = heapq.heappop(events)
            if what == "arrive":
                for q in users.get(k, ()):
                    waiting[q] -= 1
                    if waiting[q] == 0:
                        core = max(core, now) + ISSUE + sends[q].get("work", 0.0)
                        ready[q] = core
                        heapq.heappush(events, (core, count, "ready", q))
                        count += 1
            elif what == "ready":
                link = (sends[k]["axis"], sends[k]["s"])
                heapq.heappush(queue.setdefault(link, []), (rank(k), k))
                touched.append(link)
            else:
                touched.append(k)
        for link in touched:
            if queue.get(link) and busy.get(link, 0.0) <= now + 1e-6:
                _, k = heapq.heappop(queue[link])
                rate, delay = {"pair": (PAIR_RATE, PAIR_HOP), "core": (1e9, 0.0)}.get(link[0], (RATE, HOP))
                hops = sends[k].get("hops", 1)
                busy[link] = now + sends[k]["size"] * hops / rate
                begin[k] = max(ready[k], now - AHEAD)
                arrive[k] = busy[link] + delay + 0.4 * (hops - 1)
                for when, what, item in ((busy[link], "free", link), (arrive[k], "arrive", k)):
                    heapq.heappush(events, (when, count, what, item))
                    count += 1
    return sorted(sends, key=lambda k: (begin[k], k)), arrive


def gather_plan(streams):
    sends = gather_sends(streams)

    def rank(k):
        i, phase, j, s, d = k
        if phase == 4:
            return 0.0
        extra = (0, 0, 6)[i]
        if phase == 3:
            b, c = streams[i][3][1:]
            return 5 + extra + (SIZE[c] // 2 - d) + 0.3 * min(j, SIZE[b] - j)
        return extra + d

    order, arrive = timeline(sends, rank)
    return streams, sends, order, arrive


def wrap(v, n):
    return lax.rem(v + 2 * n, n)


def coords():
    u = lax.axis_index("users")
    return {"z": u // 16, "x": lax.rem(u // 4, 4), "y": lax.rem(u, 4)}


def index_of(c):
    return c["z"] * 16 + c["x"] * 4 + c["y"]


def neighbour(me, axis, s):
    c = dict(me)
    c[axis] = wrap(me[axis] + s, SIZE[axis])
    return index_of(c)


def greet(me, rep, far):
    bar = pltpu.get_barrier_semaphore()
    peers = [(axis, s) for axis in AXES for s in (1, -1)]
    peers += [(axis, s) for axis in far for s in range(2, SIZE[axis] - 1)]
    for axis, s in peers:
        pl.semaphore_signal(bar, inc=1, device_id=(neighbour(me, axis, s), rep), device_id_type=MESH)
    pl.semaphore_signal(bar, inc=1, device_id=(index_of(me), 1 - rep), device_id_type=MESH)
    pl.semaphore_wait(bar, len(peers) + 1)


def sort_keys(items, blocks):
    n = items.shape[-1]
    square = (n, n)
    key = (items * n + lax.broadcasted_iota(jnp.int32, (1, n), 1)) * 8 + blocks
    across = jnp.broadcast_to(key, square)
    down = jnp.transpose(across)
    rank = jnp.sum((down < across).astype(jnp.int32), axis=0, keepdims=True)
    rank_down = jnp.transpose(jnp.broadcast_to(rank, square))
    place = lax.broadcasted_iota(jnp.int32, square, 1)
    return jnp.sum(jnp.where(rank_down == place, down, 0), axis=0, keepdims=True)


def used_panels(items, count):
    down = jnp.transpose(jnp.broadcast_to(items, (items.shape[-1],) * 2))
    out = []
    for start in range(0, count, 128):
        panel = lax.broadcasted_iota(jnp.int32, down.shape, 1) + start
        out.append(jnp.max((down == panel).astype(jnp.int32), axis=0, keepdims=True))
    return jnp.concatenate(out, axis=1)


def gather_kernel(plans, own_ref, items_ref, blocks_ref, out_ref, keys_ref, used_ref, raw, half, other_items, send, recv, pair_recv, swap_sem, local):
    me = coords()
    rep = lax.axis_index("rep")
    bring = pltpu.make_async_copy(own_ref, raw, local.at[1])
    bring.start()
    greet(me, rep, sorted({stream[3][0] for streams, _, _, _ in plans for stream in streams}))
    bring.wait()
    half[...] = raw[...].reshape(2, 128, 256).astype(jnp.bfloat16)
    lines = pl.ds(pl.multiple_of(rep * 64, 64), 64)
    keep = pltpu.make_async_copy(half.at[:, lines], out_ref.at[me["z"], me["x"], me["y"], :, lines], local.at[0])
    keep.start()
    spot = {axis: {off: wrap(me[axis] + off, SIZE[axis]) for off in range(-(SIZE[axis] // 2), SIZE[axis] // 2 + 1)} for axis in AXES}
    close = {(axis, s): neighbour(me, axis, s) for axis in AXES for s in (1, -1)}
    pair = (index_of(me), 1 - rep)
    swap = pltpu.make_async_remote_copy(
        src_ref=items_ref, dst_ref=other_items, send_sem=swap_sem.at[0], recv_sem=swap_sem.at[1],
        device_id=pair, device_id_type=MESH,
    )

    def copy(side, key):
        streams, sends, order, arrive = plans[side]
        v = sends[key]
        panels, row0, rows, axes = streams[key[0]]
        where = []
        for axis in AXES:
            off = v["at"][axis]
            if off is not None:
                where.append(spot[axis][off])
            elif axis == axes[0] and len(v["h"]) == 1:
                where.append(pl.ds(SIZE[axis] // 2 * v["h"][0], SIZE[axis] // 2))
            else:
                where.append(slice(None))
        row = pl.ds(side * 64 + row0, rows)
        place = tuple(where) + (panels, row)
        number = order.index(key)
        arrival = recv.at[number]
        if key[1] == 4:
            target = pair
            arrival = pair_recv.at[side, number]
        elif key[1] == 1:
            target = (neighbour(me, v["axis"], v["s"] * (key[4] + 1)), rep)
        else:
            target = (close[v["axis"], v["s"]], rep)
        return pltpu.make_async_remote_copy(
            src_ref=half.at[panels, row] if not v["deps"] else out_ref.at[place],
            dst_ref=out_ref.at[place],
            send_sem=send.at[number],
            recv_sem=arrival,
            device_id=target,
            device_id_type=MESH,
        )

    def run(side):
        streams, sends, order, arrive = plans[side]
        done = set()
        kept = False
        for key in order:
            for dep in sorted(sends[key]["deps"], key=lambda k: arrive[k]):
                if dep not in done:
                    copy(side, dep).wait_recv()
                    done.add(dep)
            if sends[key]["deps"] and not kept:
                keep.wait()
                kept = True
            copy(side, key).start()
            number = order.index(key)
            if number == len(order) // 4:
                swap.start()
            if number == len(order) // 2:
                keys_ref[...] = sort_keys(items_ref[...], blocks_ref[...])
                used_ref[0:1, :] = used_panels(items_ref[...], used_ref.shape[1])
            if number == 3 * len(order) // 4:
                swap.wait()
                used_ref[1:2, :] = used_panels(other_items[...], used_ref.shape[1])
        for key in sorted(order, key=lambda k: arrive[k]):
            if key[1] != 4 and key not in done:
                copy(side, key).wait_recv()
        for key in plans[1 - side][2]:
            if key[1] == 4:
                copy(1 - side, key).wait_recv()
        for key in order:
            copy(side, key).wait_send()

    for side in range(2):
        pl.when(rep == side)(functools.partial(run, side))


def gather_panels(own, items, blocks, cid=0, name="gather_panels"):
    plans = tuple(gather_plan(streams) for streams in GATHER_STREAMS)
    count = max(len(plan[2]) for plan in plans)
    anywhere = pl.BlockSpec(memory_space=pl.ANY)
    whole = pl.BlockSpec(memory_space=pltpu.VMEM)
    return pl.pallas_call(
        functools.partial(gather_kernel, plans),
        out_shape=(
            jax.ShapeDtypeStruct((8, 4, 4, 2, 128, 256), jnp.bfloat16),
            jax.ShapeDtypeStruct(items.shape, jnp.int32),
            jax.ShapeDtypeStruct((2, 256), jnp.int32),
        ),
        in_specs=[anywhere, whole, whole],
        out_specs=(anywhere, whole, whole),
        scratch_shapes=[
            pltpu.VMEM((256, 256), jnp.float32),
            pltpu.VMEM((2, 128, 256), jnp.bfloat16),
            pltpu.VMEM(items.shape, jnp.int32),
            pltpu.SemaphoreType.DMA((count,)),
            pltpu.SemaphoreType.DMA((count,)),
            pltpu.SemaphoreType.DMA((2, count)),
            pltpu.SemaphoreType.DMA((2,)),
            pltpu.SemaphoreType.DMA((2,)),
        ],
        name=name,
        compiler_params=pltpu.CompilerParams(collective_id=cid, has_side_effects=True, vmem_limit_bytes=56 * 2**20),
    )(own, items, blocks)


REDUCE_STREAMS = (
    (slice(0, 2), 48, 16, ("y", "x", "z")),
    (slice(0, 1), 0, 48, ("y", "z", "x")),
    (slice(1, 2), 0, 48, ("x", "z", "y")),
)


def reduce_steps(n):
    out = []
    for q in range(n // 2):
        for s in (1, -1):
            out.append((s, q, n // 2 - q, ((0,) if s == 1 else (1,)) if q == 0 else (0, 1)))
    return out


def direct(i, n):
    return [(s, q, s * (q + 1)) for q in range(n // 2) for s in (1, -1) if (s == 1) == (i % 2 == 0) or q < n // 2 - 1]


def far_first(n):
    out = [n // 2]
    for d in range(n // 2 - 1, 0, -1):
        out += [d, -d]
    return out + [0]


def reduce_plan():
    tasks = {}
    zs = far_first(8)
    for n, off in enumerate(zs):
        tasks[("pair", off)] = dict(kind="pair", deps=[], size=16 * 64 * 256 * 2, rank=n)
    allz = [("pair", off) for off in zs]
    for i, (ksel, row0, rows, order) in enumerate(REDUCE_STREAMS):
        a, b, c = order
        na, nb, nc = SIZE[a], SIZE[b], SIZE[c]
        unit = (ksel.stop - ksel.start) * rows * 128 * 2
        for rank, j in enumerate(far_first(nb)):
            def shares(dist_c):
                if b == "z":
                    return [("pair", j if j != -(nb // 2) else nb // 2)]
                if c == "z":
                    return [("pair", dist_c)]
                return allz
            for s, q, e, h in reduce_steps(nc):
                at = s * e
                if at == -(nc // 2):
                    at = nc // 2
                deps = shares(at) + ([("send", i, 1, j, s, q - 1)] if q else [])
                tasks[("send", i, 1, j, s, q)] = dict(kind="send", axis=c, s=s, h=h, deps=deps, size=unit * len(h) * na, rank=rank, e=s * e)
            last = nc // 2 - 1
            tasks[("sum", i, 1, j)] = dict(kind="sum", deps=shares(0) + [("send", i, 1, j, s, last) for s in (1, -1)], size=unit * 2 * na, rank=rank)
        for s, q, e, h in reduce_steps(nb):
            line = s * e if s * e != -(nb // 2) else nb // 2
            deps = [("sum", i, 1, line)] + ([("send", i, 2, 0, s, q - 1)] if q else [])
            tasks[("send", i, 2, 0, s, q)] = dict(kind="send", axis=b, s=s, h=h, deps=deps, size=unit * len(h) * na, rank=-5, e=line)
        tasks[("sum", i, 2)] = dict(kind="sum", deps=[("sum", i, 1, 0)] + [("send", i, 2, 0, s, nb // 2 - 1) for s in (1, -1)], size=unit * 2 * na, rank=-5)
        for s, q, e in direct(i, na):
            tasks[("send", i, 3, 0, s, q)] = dict(kind="send", axis=a, s=s, h=(0, 1), deps=[("sum", i, 2)], size=4 * unit, rank=-9, e=e, hops=q + 1)
        tasks[("sum", i, 3)] = dict(kind="sum", deps=[("sum", i, 2)] + [("send", i, 3, 0, s, q) for s, q, e in direct(i, na)], size=unit * 2, rank=-9)
    for k, v in tasks.items():
        v["deps"] = list(dict.fromkeys(v["deps"]))
        if v["kind"] == "pair":
            v.update(axis="pair", s=0)
        else:
            v["work"] = v["size"] / WORK_RATE
            if v["kind"] == "sum":
                v.update(axis="core", s=k)
    pairs = [k for k in tasks if k[0] == "pair"]
    order, arrive = timeline(tasks, lambda k: reduce_rank(tasks[k], k))
    order = pairs + [k for k in order if k[0] != "pair"]
    placed, final = set(), []
    def place(k):
        if k not in placed:
            for dep in tasks[k]["deps"]:
                if dep[0] == "sum":
                    place(dep)
            placed.add(k)
            final.append(k)
    for k in order:
        place(k)
    return tasks, final, arrive


WORK_RATE = 600e3


def reduce_rank(v, k):
    if v["kind"] == "pair":
        return v["rank"]
    if v["kind"] == "sum":
        return 0.0
    return (10.0 + v["rank"], 0.0, 0.0)[k[2] - 1] + (0.0, 12.0, 12.0)[k[1]]


TASKS, TASK_ORDER, DONE_AT = reduce_plan()
SEND_INDEX = {k: n for n, k in enumerate([k for k in TASK_ORDER if k[0] != "sum"])}


def dims(i):
    ksel, row0, rows, order = REDUCE_STREAMS[i]
    return ksel.stop - ksel.start, rows, tuple(SIZE[x] for x in order)


def reduce_kernel(slots_ref, used_ref, user_ref, user_out, grad_out, mine, other, *rest):
    bufs = [dict(zip(("s1", "r1", "l1", "s2", "r2", "l2", "s3", "r3"), rest[8 * i: 8 * i + 8])) for i in range(3)]
    total, send, recv, load, last = rest[24:]
    me = coords()
    rep = lax.axis_index("rep")
    row_mine = pl.multiple_of(rep * 64, 64)
    row_other = pl.multiple_of((1 - rep) * 64, 64)
    zof = {off: wrap(me["z"] + off, 8) for off in range(-4, 5)}
    loads = {}
    for n, off in enumerate(far_first(8)):
        loads[off] = pltpu.make_async_copy(slots_ref.at[zof[off], :, :, pl.ds(row_mine, 64), :], mine.at[zof[off]], load.at[n])
        loads[off].start()
    greet(me, rep, sorted({stream[3][0] for stream in REDUCE_STREAMS}))
    pair = (index_of(me), 1 - rep)

    def remote(key):
        if key[0] == "pair":
            z = zof[key[1]]
            return pltpu.make_async_remote_copy(
                src_ref=slots_ref.at[z, :, :, pl.ds(row_other, 64), :], dst_ref=other.at[z],
                send_sem=send.at[SEND_INDEX[key]], recv_sem=recv.at[SEND_INDEX[key]], device_id=pair, device_id_type=MESH)
        _, i, phase, j, s, q = key
        v = TASKS[key]
        nb = dims(i)[2][1]
        cols = pl.ds(0, 256) if len(v["h"]) == 2 else pl.ds(128 * v["h"][0], 128)
        side = 0 if s == 1 else 1
        at = (j % nb, side, q) if phase == 1 else (side, q)
        tail = (slice(None),) * (2 if phase == 3 else 3) + (cols,)
        return pltpu.make_async_remote_copy(
            src_ref=bufs[i]["s%d" % phase].at[at + tail], dst_ref=bufs[i]["r%d" % phase].at[at + tail],
            send_sem=send.at[SEND_INDEX[key]], recv_sem=recv.at[SEND_INDEX[key]],
            device_id=(neighbour(me, v["axis"], v["e"] if phase == 3 else s), rep), device_id_type=MESH)

    def share(i, offs, n, cols):
        ksel, row0, rows, order = REDUCE_STREAMS[i]
        a, b, c = order
        where = {b: wrap(me[b] + offs[0], SIZE[b]), c: wrap(me[c] + offs[1], SIZE[c]), a: n}
        owner = index_of(where)
        place = (where["z"], where["x"], where["y"], pl.ds(row0, rows), cols)
        x = mine[place].astype(jnp.float32)
        y = other[place].astype(jnp.float32)
        out = []
        for k in range(ksel.start, ksel.stop):
            ux = used_ref[0, owner * 2 + k] > 0
            uy = used_ref[1, owner * 2 + k] > 0
            out.append(jnp.where(ux, x, 0.0) + jnp.where(uy, y, 0.0))
        return out

    def work(key):
        v = TASKS[key]
        i = key[1]
        kk, rows, (na, nb, nc) = dims(i)
        buf = bufs[i]
        if key[0] == "send":
            _, i, phase, j, s, q = key
            side = 0 if s == 1 else 1
            if phase == 3:
                n = wrap(me[REDUCE_STREAMS[i][3][0]] + v["e"], na)
                buf["s3"][side, q] = buf["l2"][n]
                return
            for h in ((0, 1) if (q == 1) else (None,)):
                cols = pl.ds(128 * h, 128) if h is not None else (pl.ds(0, 256) if len(v["h"]) == 2 else pl.ds(128 * v["h"][0], 128))
                got = q >= 2 or (q == 1 and h == side)

                def body(n, _, cols=cols, got=got):
                    if phase == 1:
                        parts = share(i, (j, v["e"]), n, cols)
                    elif phase == 2:
                        parts = [buf["l1"][v["e"] % nb, n, k, :, cols] for k in range(kk)]
                    for k in range(kk):
                        x = parts[k]
                        if phase == 1:
                            if got:
                                x = x + buf["r1"][j % nb, side, q - 1, n, k, :, cols].astype(jnp.float32)
                            buf["s1"][j % nb, side, q, n, k, :, cols] = x.astype(jnp.bfloat16)
                        else:
                            if got:
                                x = x + buf["r2"][side, q - 1, n, k, :, cols].astype(jnp.float32)
                            buf["s2"][side, q, n, k, :, cols] = x.astype(jnp.bfloat16)
                    return 0

                lax.fori_loop(0, na, body, 0)
            return
        phase = key[2]
        end = {1: nc, 2: nb, 3: na}[phase] // 2 - 1
        full = pl.ds(0, 256)
        if phase == 1:
            j = key[3]

            def body(n, _):
                parts = share(i, (j, 0), n, full)
                for k in range(kk):
                    x = parts[k]
                    for side in range(2):
                        x = x + buf["r1"][j % nb, side, end, n, k].astype(jnp.float32)
                    buf["l1"][j % nb, n, k] = x
                return 0

            lax.fori_loop(0, na, body, 0)
        elif phase == 2:

            def body(n, _):
                for k in range(kk):
                    x = buf["l1"][0, n, k]
                    for side in range(2):
                        x = x + buf["r2"][side, end, n, k].astype(jnp.float32)
                    buf["l2"][n, k] = x
                return 0

            lax.fori_loop(0, na, body, 0)
        else:
            ksel, row0, rows, order = REDUCE_STREAMS[i]
            n = me[order[0]]
            for k in range(kk):
                x = buf["l2"][n, k]
                for s, q, e in direct(i, na):
                    x = x + buf["r3"][0 if s == 1 else 1, q, k]
                total[ksel.start + k, pl.ds(row0, rows), :] = x

    swap = pltpu.make_async_remote_copy(
        src_ref=user_ref, dst_ref=user_out, send_sem=last.at[0], recv_sem=last.at[1], device_id=pair, device_id_type=MESH)
    done = set()
    swapped = False
    for key in TASK_ORDER:
        if key[0] == "pair":
            remote(key).start()
            continue
        if not swapped:
            swap.start()
            swapped = True
        for dep in sorted(TASKS[key]["deps"], key=lambda k: DONE_AT[k]):
            if dep[0] == "sum" or dep in done:
                continue
            if dep[0] == "pair":
                loads[dep[1]].wait()
            remote(dep).wait_recv()
            done.add(dep)
        work(key)
        if key[0] == "send":
            remote(key).start()
    keep = pltpu.make_async_copy(total, grad_out.at[:, pl.ds(row_mine, 64), :], last.at[2])
    give = pltpu.make_async_remote_copy(
        src_ref=total, dst_ref=grad_out.at[:, pl.ds(row_mine, 64), :], send_sem=last.at[3], recv_sem=last.at[4],
        device_id=pair, device_id_type=MESH)
    keep.start()
    give.start()
    for key in SEND_INDEX:
        if key not in done:
            if key[0] == "pair":
                loads[key[1]].wait()
            remote(key).wait_recv()
        remote(key).wait_send()
    swap.wait()
    keep.wait()
    give.wait()


def reduce_parts(slots, used, user_part, cid=1, name='reduce_parts'):
    scratch = [pltpu.VMEM((8, 4, 4, 64, 256), jnp.bfloat16)] * 2
    for i in range(3):
        kk, rows, (na, nb, nc) = dims(i)
        unit = (kk, rows, 256)
        scratch += [pltpu.VMEM((nb, 2, nc // 2, na) + unit, jnp.bfloat16)] * 2
        scratch += [pltpu.VMEM((nb, na) + unit, jnp.float32)]
        scratch += [pltpu.VMEM((2, nb // 2, na) + unit, jnp.bfloat16)] * 2
        scratch += [pltpu.VMEM((na,) + unit, jnp.float32)]
        scratch += [pltpu.VMEM((2, na // 2) + unit, jnp.float32)] * 2
    count = len(SEND_INDEX)
    scratch += [
        pltpu.VMEM((2, 64, 256), jnp.float32),
        pltpu.SemaphoreType.DMA((count,)), pltpu.SemaphoreType.DMA((count,)),
        pltpu.SemaphoreType.DMA((8,)), pltpu.SemaphoreType.DMA((5,)),
    ]
    anywhere = pl.BlockSpec(memory_space=pl.ANY)
    return pl.pallas_call(
        reduce_kernel,
        out_shape=(
            jax.ShapeDtypeStruct(user_part.shape, jnp.float32),
            jax.ShapeDtypeStruct((2, 128, 256), jnp.float32),
        ),
        in_specs=[anywhere, pl.BlockSpec(memory_space=pltpu.SMEM), anywhere],
        out_specs=(anywhere, anywhere),
        scratch_shapes=scratch,
        name=name,
        compiler_params=pltpu.CompilerParams(collective_id=cid, has_side_effects=True, vmem_limit_bytes=56 * 2**20),
    )(slots.reshape(8, 4, 4, 128, 256), used, user_part)


GROUP, RING = 16, 32


def tiles_kernel(keys_ref, panels_ref, counts_ref, users_ref, slots_out, user_out, half, raw, usem, vbuf, cbuf, acc, stage, vsem, csem, ssem):
    tiles = counts_ref.shape[0]

    def key(i):
        return keys_ref[jnp.clip(i, 0, tiles - 1)]

    def owner(i):
        return lax.shift_right_logical(key(i), 11)

    def fetch(i):
        k = key(i)
        slot = lax.rem(i, RING)
        item = lax.shift_right_logical(k, 10)
        tile = lax.rem(lax.shift_right_logical(k, 3), 128)
        return (
            pltpu.make_async_copy(panels_ref.at[item], vbuf.at[slot], vsem.at[slot]),
            pltpu.make_async_copy(counts_ref.at[tile], cbuf.at[slot], csem.at[slot]),
        )

    def put(i):
        slot = lax.rem(i, RING)
        return pltpu.make_async_copy(stage.at[slot], slots_out.at[owner(i)], ssem.at[slot])

    def is_last(i):
        return (i == tiles - 1) | (owner(i) != owner(i + 1))

    def start(i, _):
        for c in fetch(i):
            c.start()
        return 0

    bring = pltpu.make_async_copy(users_ref, raw, usem)
    bring.start()
    lax.fori_loop(0, RING, start, 0)
    bring.wait()
    half[...] = raw[...].astype(jnp.bfloat16)
    user_out[...] = jnp.zeros_like(user_out)
    acc[...] = jnp.zeros_like(acc)

    def group(g, _):
        base = g * GROUP
        for n in range(GROUP):
            for c in fetch(base + n):
                c.wait()

        @pl.when(base >= RING)
        def _():
            for n in range(GROUP):

                @pl.when(is_last(base + n - RING))
                def _():
                    put(base + n - RING).wait()

        errs = []
        for n in range(GROUP):
            i = base + n
            slot = lax.rem(i, RING)
            block = lax.rem(key(i), 8)
            u = half[block]
            v = vbuf[slot]
            predicted = lax.dot_general(u, v, (((1,), (1,)), ((), ())), preferred_element_type=jnp.float32)
            amount = cbuf[slot].astype(jnp.float32)
            weight = amount * (0.5 / 64.0) + 1.0 / 64.0
            errs.append((weight * (predicted - jnp.where(amount > 0, 1.0, 0.0))).astype(jnp.bfloat16))
        for n in range(GROUP):
            i = base + n
            slot = lax.rem(i, RING)
            block = lax.rem(key(i), 8)
            first = (i == 0) | (owner(i) != owner(i - 1))
            item_part = lax.dot_general(errs[n], half[block], (((0,), (0,)), ((), ())), preferred_element_type=jnp.float32)
            total = jnp.where(first, 0.0, acc[...]) + item_part
            acc[...] = total
            stage[slot] = total.astype(jnp.bfloat16)
            user_out[block] += jnp.dot(errs[n], vbuf[slot], preferred_element_type=jnp.float32)
        for n in range(GROUP):
            i = base + n

            @pl.when(is_last(i))
            def _():
                put(i).start()

        @pl.when(base + RING < tiles)
        def _():
            for n in range(GROUP):
                for c in fetch(base + n + RING):
                    c.start()

        return 0

    lax.fori_loop(0, tiles // GROUP, group, 0)

    def finish(n, _):
        i = tiles - RING + n

        @pl.when(is_last(i))
        def _():
            put(i).wait()

        return 0

    lax.fori_loop(0, RING, finish, 0)


def tile_parts(keys, panels, counts, users):
    anywhere = pl.BlockSpec(memory_space=pl.ANY)
    whole = pl.BlockSpec(memory_space=pltpu.VMEM)
    return pl.pallas_call(
        tiles_kernel,
        out_shape=(
            jax.ShapeDtypeStruct((128, 128, 256), jnp.bfloat16),
            jax.ShapeDtypeStruct((8, 128, 256), jnp.float32),
        ),
        in_specs=[pl.BlockSpec(memory_space=pltpu.SMEM), anywhere, anywhere, anywhere],
        out_specs=(anywhere, whole),
        scratch_shapes=[
            pltpu.VMEM((8, 128, 256), jnp.bfloat16),
            pltpu.VMEM((8, 128, 256), jnp.float32),
            pltpu.SemaphoreType.DMA,
            pltpu.VMEM((RING, 128, 256), jnp.bfloat16),
            pltpu.VMEM((RING, 128, 128), jnp.bfloat16),
            pltpu.VMEM((128, 256), jnp.float32),
            pltpu.VMEM((RING, 128, 256), jnp.bfloat16),
            pltpu.SemaphoreType.DMA((RING,)),
            pltpu.SemaphoreType.DMA((RING,)),
            pltpu.SemaphoreType.DMA((RING,)),
        ],
        name="tile_parts",
        compiler_params=pltpu.CompilerParams(vmem_limit_bytes=58 * 2**20),
        cost_estimate=pl.CostEstimate(flops=128 * 6 * 128 * 128 * 256, bytes_accessed=26 * 2**20, transcendentals=0),
    )(keys, panels, counts, users)


def adagrad_kernel(part, other, users, user_accum, grad, items, item_accum, new_users, new_user_accum, new_items, new_item_accum):
    for g, factors, accum, new, new_accum in (
        (part[...] + other[...], users, user_accum, new_users, new_user_accum),
        (grad[...], items, item_accum, new_items, new_item_accum),
    ):
        total = accum[...] + g * g
        new_accum[...] = total
        new[...] = factors[...] - g / jnp.sqrt(total)


def adagrad(part, other, users, user_accum, grad, items, item_accum, steps=4):
    def rows(x):
        return pl.BlockSpec((x.shape[0] // steps, x.shape[1]), lambda n: (n, 0))

    args = (part, other, users, user_accum, grad, items, item_accum)
    outs = (users, user_accum, items, item_accum)
    return pl.pallas_call(
        adagrad_kernel,
        grid=(steps,),
        out_shape=tuple(jax.ShapeDtypeStruct(x.shape, x.dtype) for x in outs),
        in_specs=[rows(x) for x in args],
        out_specs=tuple(rows(x) for x in outs),
        name="adagrad",
        compiler_params=pltpu.CompilerParams(vmem_limit_bytes=56 * 2**20),
    )(*args)


def local(user_factors, user_accum, item_factors, item_accum, tile_counts, tile_user, tile_item, send_list):
    counts = tile_counts[0, 0]
    panels, keys, used = gather_panels(item_factors, tile_item[0], tile_user[0])
    slots, user_part = tile_parts(keys[0], panels.reshape(256, 128, 256), counts, user_factors.reshape(8, 128, 256))
    other_user, item_grad = reduce_parts(slots, used, user_part.reshape(1024, 256))
    return adagrad(
        user_part.reshape(1024, 256), other_user, user_factors, user_accum,
        item_grad.reshape(256, 256), item_factors, item_accum,
    )


def solution(mesh):
    rows = P("users", None)
    return jax.shard_map(
        local,
        mesh=mesh,
        in_specs=(rows, rows, rows, rows, P("users", "rep", None, None, None), P("users", "rep", None), P("users", "rep", None), P("users", "rep", None)),
        out_specs=(rows, rows, rows, rows),
        check_vma=False,
    )
```

```python
import functools
import heapq

import jax
import jax.numpy as jnp
from jax import lax
from jax.experimental import pallas as pl
from jax.experimental.pallas import tpu as pltpu
from jax.sharding import PartitionSpec as P

MESH = pl.DeviceIdType.MESH
AXES = ("z", "x", "y")
SIZE = {"z": 8, "x": 4, "y": 4}
GATHER_STREAMS = (
    (
        (slice(0, 2), 48, 16, ("x", "y", "z")),
        (slice(0, 1), 0, 48, ("y", "z", "x")),
        (slice(1, 2), 0, 48, ("x", "z", "y")),
    ),
    (
        (slice(1, 2), 48, 16, ("x", "y", "z")),
        (slice(0, 1), 0, 64, ("y", "z", "x")),
        (slice(1, 2), 0, 48, ("x", "z", "y")),
    ),
)
RATE, PAIR_RATE, HOP, PAIR_HOP, ISSUE, AHEAD = 43e3, 500e3, 1.7, 0.8, 0.07, 2.5


def signed(j, n):
    return j if j <= n // 2 else j - n


def ring_steps(n):
    out = []
    for d in range(n // 2):
        for s in (1, -1):
            last = d == n // 2 - 1
            out.append((s, d, ((0,) if s == 1 else (1,)) if last else (0, 1)))
    return out


def gather_sends(streams):
    sends = {}
    for i, (panels, row0, rows, order) in enumerate(streams):
        a, b, c = order
        unit = (panels.stop - panels.start) * rows * 128 * 2
        na, nb, nc = SIZE[a], SIZE[b], SIZE[c]
        first = [(s, d) for d in range(na // 2) for s in (1, -1) if (s == 1) == (i % 2 == 0) or d < na // 2 - 1]
        near = [(i, 1, 0, s, d) for s, d in first]

        def add(key, axis, h, deps, size, at):
            sends[key] = dict(axis=axis, s=key[3], h=h, deps=deps, size=size, at=at)

        for s, d in first:
            add((i, 1, 0, s, d), a, (0, 1), [], unit * 2, {a: 0, b: 0, c: 0})
            sends[i, 1, 0, s, d].update(hops=d + 1)
        for s, d, h in ring_steps(nb):
            deps = near if d == 0 else [(i, 2, 0, s, d - 1)]
            add((i, 2, 0, s, d), b, h, deps, unit * len(h) * na, {a: None, b: -s * d, c: 0})
        for j in range(nb):
            off = signed(j, nb)
            if off == 0:
                line = near
            elif off == nb // 2:
                line = [(i, 2, 0, s, nb // 2 - 1) for s in (1, -1)]
            else:
                line = [(i, 2, 0, -1 if off > 0 else 1, abs(off) - 1)]
            for s, d, h in ring_steps(nc):
                deps = line if d == 0 else [(i, 3, j, s, d - 1)]
                add((i, 3, j, s, d), c, h, deps, unit * len(h) * na, {a: None, b: off, c: -s * d})
            deps = line + [(i, 3, j, s, d) for s, d, h in ring_steps(nc)]
            add((i, 4, j, 0, 0), "pair", (0, 1), deps, unit * 2 * na * nc, {a: None, b: off, c: None})
    return sends


def timeline(sends, rank):
    users, waiting, ready, begin, arrive, queue, busy, events = {}, {}, {}, {}, {}, {}, {}, []
    core, count = 0.0, 0
    for k, v in sends.items():
        waiting[k] = len(v["deps"])
        for dep in v["deps"]:
            users.setdefault(dep, []).append(k)
        if not v["deps"]:
            ready[k] = 0.0
            heapq.heappush(events, (0.0, count, "ready", k))
            count += 1
    while events:
        now = events[0][0]
        touched = []
        while events and events[0][0] <= now + 1e-9:
            _, _, what, k = heapq.heappop(events)
            if what == "arrive":
                for q in users.get(k, ()):
                    waiting[q] -= 1
                    if waiting[q] == 0:
                        core = max(core, now) + ISSUE + sends[q].get("work", 0.0)
                        ready[q] = core
                        heapq.heappush(events, (core, count, "ready", q))
                        count += 1
            elif what == "ready":
                link = (sends[k]["axis"], sends[k]["s"])
                heapq.heappush(queue.setdefault(link, []), (rank(k), k))
                touched.append(link)
            else:
                touched.append(k)
        for link in touched:
            if queue.get(link) and busy.get(link, 0.0) <= now + 1e-6:
                _, k = heapq.heappop(queue[link])
                rate, delay = {"pair": (PAIR_RATE, PAIR_HOP), "core": (1e9, 0.0)}.get(link[0], (RATE, HOP))
                hops = sends[k].get("hops", 1)
                busy[link] = now + sends[k]["size"] * hops / rate
                begin[k] = max(ready[k], now - AHEAD)
                arrive[k] = busy[link] + delay + 0.4 * (hops - 1)
                for when, what, item in ((busy[link], "free", link), (arrive[k], "arrive", k)):
                    heapq.heappush(events, (when, count, what, item))
                    count += 1
    return sorted(sends, key=lambda k: (begin[k], k)), arrive


def gather_plan(streams):
    sends = gather_sends(streams)

    def rank(k):
        i, phase, j, s, d = k
        if phase == 4:
            return 0.0
        extra = (0, 6, 0)[i]
        if phase == 3:
            return 20 + extra - 0.5 * (SIZE[streams[i][3][2]] // 2 - d)
        return extra - d

    order, arrive = timeline(sends, rank)
    return streams, sends, order, arrive


def wrap(v, n):
    return lax.rem(v + 2 * n, n)


def coords():
    u = lax.axis_index("users")
    return {"z": u // 16, "x": lax.rem(u // 4, 4), "y": lax.rem(u, 4)}


def index_of(c):
    return c["z"] * 16 + c["x"] * 4 + c["y"]


def neighbour(me, axis, s):
    c = dict(me)
    c[axis] = wrap(me[axis] + s, SIZE[axis])
    return index_of(c)


def greet(me, rep, far):
    bar = pltpu.get_barrier_semaphore()
    peers = [(axis, s) for axis in AXES for s in (1, -1)]
    peers += [(axis, s) for axis in far for s in range(2, SIZE[axis] - 1)]
    for axis, s in peers:
        pl.semaphore_signal(bar, inc=1, device_id=(neighbour(me, axis, s), rep), device_id_type=MESH)
    pl.semaphore_signal(bar, inc=1, device_id=(index_of(me), 1 - rep), device_id_type=MESH)
    pl.semaphore_wait(bar, len(peers) + 1)


def sort_keys(items, blocks):
    n = items.shape[-1]
    square = (n, n)
    key = (items * n + lax.broadcasted_iota(jnp.int32, (1, n), 1)) * 8 + blocks
    across = jnp.broadcast_to(key, square)
    down = jnp.transpose(across)
    rank = jnp.sum((down < across).astype(jnp.int32), axis=0, keepdims=True)
    rank_down = jnp.transpose(jnp.broadcast_to(rank, square))
    place = lax.broadcasted_iota(jnp.int32, square, 1)
    return jnp.sum(jnp.where(rank_down == place, down, 0), axis=0, keepdims=True)


def used_panels(items, count):
    down = jnp.transpose(jnp.broadcast_to(items, (items.shape[-1],) * 2))
    out = []
    for start in range(0, count, 128):
        panel = lax.broadcasted_iota(jnp.int32, down.shape, 1) + start
        out.append(jnp.max((down == panel).astype(jnp.int32), axis=0, keepdims=True))
    return jnp.concatenate(out, axis=1)


def gather_kernel(plans, own_ref, items_ref, blocks_ref, out_ref, keys_ref, used_ref, raw, half, other_items, send, recv, pair_recv, swap_sem, local):
    me = coords()
    rep = lax.axis_index("rep")
    bring = pltpu.make_async_copy(own_ref, raw, local.at[1])
    bring.start()
    greet(me, rep, sorted({stream[3][0] for streams, _, _, _ in plans for stream in streams}))
    bring.wait()
    half[...] = raw[...].reshape(2, 128, 256).astype(jnp.bfloat16)
    lines = pl.ds(pl.multiple_of(rep * 64, 64), 64)
    keep = pltpu.make_async_copy(half.at[:, lines], out_ref.at[me["z"], me["x"], me["y"], :, lines], local.at[0])
    keep.start()
    spot = {axis: {off: wrap(me[axis] + off, SIZE[axis]) for off in range(-(SIZE[axis] // 2), SIZE[axis] // 2 + 1)} for axis in AXES}
    close = {(axis, s): neighbour(me, axis, s) for axis in AXES for s in (1, -1)}
    pair = (index_of(me), 1 - rep)
    swap = pltpu.make_async_remote_copy(
        src_ref=items_ref, dst_ref=other_items, send_sem=swap_sem.at[0], recv_sem=swap_sem.at[1],
        device_id=pair, device_id_type=MESH,
    )

    def copy(side, key):
        streams, sends, order, arrive = plans[side]
        v = sends[key]
        panels, row0, rows, axes = streams[key[0]]
        where = []
        for axis in AXES:
            off = v["at"][axis]
            if off is not None:
                where.append(spot[axis][off])
            elif axis == axes[0] and len(v["h"]) == 1:
                where.append(pl.ds(SIZE[axis] // 2 * v["h"][0], SIZE[axis] // 2))
            else:
                where.append(slice(None))
        row = pl.ds(side * 64 + row0, rows)
        place = tuple(where) + (panels, row)
        number = order.index(key)
        arrival = recv.at[number]
        if key[1] == 4:
            target = pair
            arrival = pair_recv.at[side, number]
        elif key[1] == 1:
            target = (neighbour(me, v["axis"], v["s"] * (key[4] + 1)), rep)
        else:
            target = (close[v["axis"], v["s"]], rep)
        return pltpu.make_async_remote_copy(
            src_ref=half.at[panels, row] if not v["deps"] else out_ref.at[place],
            dst_ref=out_ref.at[place],
            send_sem=send.at[number],
            recv_sem=arrival,
            device_id=target,
            device_id_type=MESH,
        )

    def run(side):
        streams, sends, order, arrive = plans[side]
        done = set()
        kept = False
        for key in order:
            for dep in sorted(sends[key]["deps"], key=lambda k: arrive[k]):
                if dep not in done:
                    copy(side, dep).wait_recv()
                    done.add(dep)
            if sends[key]["deps"] and not kept:
                keep.wait()
                kept = True
            copy(side, key).start()
            number = order.index(key)
            if number == len(order) // 4:
                swap.start()
            if number == len(order) // 2:
                keys_ref[...] = sort_keys(items_ref[...], blocks_ref[...])
                used_ref[0:1, :] = used_panels(items_ref[...], used_ref.shape[1])
            if number == 3 * len(order) // 4:
                swap.wait()
                used_ref[1:2, :] = used_panels(other_items[...], used_ref.shape[1])
        for key in sorted(order, key=lambda k: arrive[k]):
            if key[1] != 4 and key not in done:
                copy(side, key).wait_recv()
        for key in plans[1 - side][2]:
            if key[1] == 4:
                copy(1 - side, key).wait_recv()
        for key in order:
            copy(side, key).wait_send()

    for side in range(2):
        pl.when(rep == side)(functools.partial(run, side))


def gather_panels(own, items, blocks, cid=0, name="gather_panels"):
    plans = tuple(gather_plan(streams) for streams in GATHER_STREAMS)
    count = max(len(plan[2]) for plan in plans)
    anywhere = pl.BlockSpec(memory_space=pl.ANY)
    whole = pl.BlockSpec(memory_space=pltpu.VMEM)
    return pl.pallas_call(
        functools.partial(gather_kernel, plans),
        out_shape=(
            jax.ShapeDtypeStruct((8, 4, 4, 2, 128, 256), jnp.bfloat16),
            jax.ShapeDtypeStruct(items.shape, jnp.int32),
            jax.ShapeDtypeStruct((2, 256), jnp.int32),
        ),
        in_specs=[anywhere, whole, whole],
        out_specs=(anywhere, whole, whole),
        scratch_shapes=[
            pltpu.VMEM((256, 256), jnp.float32),
            pltpu.VMEM((2, 128, 256), jnp.bfloat16),
            pltpu.VMEM(items.shape, jnp.int32),
            pltpu.SemaphoreType.DMA((count,)),
            pltpu.SemaphoreType.DMA((count,)),
            pltpu.SemaphoreType.DMA((2, count)),
            pltpu.SemaphoreType.DMA((2,)),
            pltpu.SemaphoreType.DMA((2,)),
        ],
        name=name,
        compiler_params=pltpu.CompilerParams(collective_id=cid, has_side_effects=True, vmem_limit_bytes=56 * 2**20),
    )(own, items, blocks)


REDUCE_STREAMS = (
    (slice(0, 2), 48, 16, ("y", "x", "z")),
    (slice(0, 1), 0, 48, ("y", "z", "x")),
    (slice(1, 2), 0, 48, ("x", "z", "y")),
)


def reduce_steps(n):
    out = []
    for q in range(n // 2):
        for s in (1, -1):
            out.append((s, q, n // 2 - q, ((0,) if s == 1 else (1,)) if q == 0 else (0, 1)))
    return out


def direct(i, n):
    return [(s, q, s * (q + 1)) for q in range(n // 2) for s in (1, -1) if (s == 1) == (i % 2 == 0) or q < n // 2 - 1]


def far_first(n):
    out = [n // 2]
    for d in range(n // 2 - 1, 0, -1):
        out += [d, -d]
    return out + [0]


def reduce_plan():
    tasks = {}
    zs = far_first(8)
    for n, off in enumerate(zs):
        tasks[("pair", off)] = dict(kind="pair", deps=[], size=16 * 64 * 256 * 2, rank=n)
    allz = [("pair", off) for off in zs]
    for i, (ksel, row0, rows, order) in enumerate(REDUCE_STREAMS):
        a, b, c = order
        na, nb, nc = SIZE[a], SIZE[b], SIZE[c]
        unit = (ksel.stop - ksel.start) * rows * 128 * 2
        for rank, j in enumerate(far_first(nb)):
            def shares(dist_c):
                if b == "z":
                    return [("pair", j if j != -(nb // 2) else nb // 2)]
                if c == "z":
                    return [("pair", dist_c)]
                return allz
            for s, q, e, h in reduce_steps(nc):
                at = s * e
                if at == -(nc // 2):
                    at = nc // 2
                deps = shares(at) + ([("send", i, 1, j, s, q - 1)] if q else [])
                tasks[("send", i, 1, j, s, q)] = dict(kind="send", axis=c, s=s, h=h, deps=deps, size=unit * len(h) * na, rank=rank, e=s * e)
            last = nc // 2 - 1
            tasks[("sum", i, 1, j)] = dict(kind="sum", deps=shares(0) + [("send", i, 1, j, s, last) for s in (1, -1)], size=unit * 2 * na, rank=rank)
        for s, q, e, h in reduce_steps(nb):
            line = s * e if s * e != -(nb // 2) else nb // 2
            deps = [("sum", i, 1, line)] + ([("send", i, 2, 0, s, q - 1)] if q else [])
            tasks[("send", i, 2, 0, s, q)] = dict(kind="send", axis=b, s=s, h=h, deps=deps, size=unit * len(h) * na, rank=-5, e=line)
        tasks[("sum", i, 2)] = dict(kind="sum", deps=[("sum", i, 1, 0)] + [("send", i, 2, 0, s, nb // 2 - 1) for s in (1, -1)], size=unit * 2 * na, rank=-5)
        for s, q, e in direct(i, na):
            tasks[("send", i, 3, 0, s, q)] = dict(kind="send", axis=a, s=s, h=(0, 1), deps=[("sum", i, 2)], size=4 * unit, rank=-9, e=e, hops=q + 1)
        tasks[("sum", i, 3)] = dict(kind="sum", deps=[("sum", i, 2)] + [("send", i, 3, 0, s, q) for s, q, e in direct(i, na)], size=unit * 2, rank=-9)
    for k, v in tasks.items():
        v["deps"] = list(dict.fromkeys(v["deps"]))
        if v["kind"] == "pair":
            v.update(axis="pair", s=0)
        else:
            v["work"] = v["size"] / WORK_RATE
            if v["kind"] == "sum":
                v.update(axis="core", s=k)
    pairs = [k for k in tasks if k[0] == "pair"]
    order, arrive = timeline(tasks, lambda k: reduce_rank(tasks[k], k))
    order = pairs + [k for k in order if k[0] != "pair"]
    placed, final = set(), []
    def place(k):
        if k not in placed:
            for dep in tasks[k]["deps"]:
                if dep[0] == "sum":
                    place(dep)
            placed.add(k)
            final.append(k)
    for k in order:
        place(k)
    return tasks, final, arrive


WORK_RATE = 600e3


def reduce_rank(v, k):
    if v["kind"] == "pair":
        return v["rank"]
    if v["kind"] == "sum":
        return 0.0
    return (10.0 + v["rank"], 0.0, 0.0)[k[2] - 1] + (0.0, 12.0, 12.0)[k[1]]


TASKS, TASK_ORDER, DONE_AT = reduce_plan()
SEND_INDEX = {k: n for n, k in enumerate([k for k in TASK_ORDER if k[0] != "sum"])}


def dims(i):
    ksel, row0, rows, order = REDUCE_STREAMS[i]
    return ksel.stop - ksel.start, rows, tuple(SIZE[x] for x in order)


def reduce_kernel(slots_ref, used_ref, user_ref, user_out, grad_out, mine, other, *rest):
    bufs = [dict(zip(("s1", "r1", "l1", "s2", "r2", "l2", "s3", "r3"), rest[8 * i: 8 * i + 8])) for i in range(3)]
    total, send, recv, load, last = rest[24:]
    me = coords()
    rep = lax.axis_index("rep")
    row_mine = pl.multiple_of(rep * 64, 64)
    row_other = pl.multiple_of((1 - rep) * 64, 64)
    zof = {off: wrap(me["z"] + off, 8) for off in range(-4, 5)}
    loads = {}
    for n, off in enumerate(far_first(8)):
        loads[off] = pltpu.make_async_copy(slots_ref.at[zof[off], :, :, pl.ds(row_mine, 64), :], mine.at[zof[off]], load.at[n])
        loads[off].start()
    greet(me, rep, sorted({stream[3][0] for stream in REDUCE_STREAMS}))
    pair = (index_of(me), 1 - rep)

    def remote(key):
        if key[0] == "pair":
            z = zof[key[1]]
            return pltpu.make_async_remote_copy(
                src_ref=slots_ref.at[z, :, :, pl.ds(row_other, 64), :], dst_ref=other.at[z],
                send_sem=send.at[SEND_INDEX[key]], recv_sem=recv.at[SEND_INDEX[key]], device_id=pair, device_id_type=MESH)
        _, i, phase, j, s, q = key
        v = TASKS[key]
        nb = dims(i)[2][1]
        cols = pl.ds(0, 256) if len(v["h"]) == 2 else pl.ds(128 * v["h"][0], 128)
        side = 0 if s == 1 else 1
        at = (j % nb, side, q) if phase == 1 else (side, q)
        tail = (slice(None),) * (2 if phase == 3 else 3) + (cols,)
        return pltpu.make_async_remote_copy(
            src_ref=bufs[i]["s%d" % phase].at[at + tail], dst_ref=bufs[i]["r%d" % phase].at[at + tail],
            send_sem=send.at[SEND_INDEX[key]], recv_sem=recv.at[SEND_INDEX[key]],
            device_id=(neighbour(me, v["axis"], v["e"] if phase == 3 else s), rep), device_id_type=MESH)

    def share(i, offs, n, cols):
        ksel, row0, rows, order = REDUCE_STREAMS[i]
        a, b, c = order
        where = {b: wrap(me[b] + offs[0], SIZE[b]), c: wrap(me[c] + offs[1], SIZE[c]), a: n}
        owner = index_of(where)
        place = (where["z"], where["x"], where["y"], pl.ds(row0, rows), cols)
        x = mine[place].astype(jnp.float32)
        y = other[place].astype(jnp.float32)
        out = []
        for k in range(ksel.start, ksel.stop):
            ux = used_ref[0, owner * 2 + k] > 0
            uy = used_ref[1, owner * 2 + k] > 0
            out.append(jnp.where(ux, x, 0.0) + jnp.where(uy, y, 0.0))
        return out

    def work(key):
        v = TASKS[key]
        i = key[1]
        kk, rows, (na, nb, nc) = dims(i)
        buf = bufs[i]
        if key[0] == "send":
            _, i, phase, j, s, q = key
            side = 0 if s == 1 else 1
            if phase == 3:
                n = wrap(me[REDUCE_STREAMS[i][3][0]] + v["e"], na)
                buf["s3"][side, q] = buf["l2"][n]
                return
            for h in ((0, 1) if (q == 1) else (None,)):
                cols = pl.ds(128 * h, 128) if h is not None else (pl.ds(0, 256) if len(v["h"]) == 2 else pl.ds(128 * v["h"][0], 128))
                got = q >= 2 or (q == 1 and h == side)

                def body(n, _, cols=cols, got=got):
                    if phase == 1:
                        parts = share(i, (j, v["e"]), n, cols)
                    elif phase == 2:
                        parts = [buf["l1"][v["e"] % nb, n, k, :, cols] for k in range(kk)]
                    for k in range(kk):
                        x = parts[k]
                        if phase == 1:
                            if got:
                                x = x + buf["r1"][j % nb, side, q - 1, n, k, :, cols].astype(jnp.float32)
                            buf["s1"][j % nb, side, q, n, k, :, cols] = x.astype(jnp.bfloat16)
                        else:
                            if got:
                                x = x + buf["r2"][side, q - 1, n, k, :, cols].astype(jnp.float32)
                            buf["s2"][side, q, n, k, :, cols] = x.astype(jnp.bfloat16)
                    return 0

                lax.fori_loop(0, na, body, 0)
            return
        phase = key[2]
        end = {1: nc, 2: nb, 3: na}[phase] // 2 - 1
        full = pl.ds(0, 256)
        if phase == 1:
            j = key[3]

            def body(n, _):
                parts = share(i, (j, 0), n, full)
                for k in range(kk):
                    x = parts[k]
                    for side in range(2):
                        x = x + buf["r1"][j % nb, side, end, n, k].astype(jnp.float32)
                    buf["l1"][j % nb, n, k] = x
                return 0

            lax.fori_loop(0, na, body, 0)
        elif phase == 2:

            def body(n, _):
                for k in range(kk):
                    x = buf["l1"][0, n, k]
                    for side in range(2):
                        x = x + buf["r2"][side, end, n, k].astype(jnp.float32)
                    buf["l2"][n, k] = x
                return 0

            lax.fori_loop(0, na, body, 0)
        else:
            ksel, row0, rows, order = REDUCE_STREAMS[i]
            n = me[order[0]]
            for k in range(kk):
                x = buf["l2"][n, k]
                for s, q, e in direct(i, na):
                    x = x + buf["r3"][0 if s == 1 else 1, q, k]
                total[ksel.start + k, pl.ds(row0, rows), :] = x

    swap = pltpu.make_async_remote_copy(
        src_ref=user_ref, dst_ref=user_out, send_sem=last.at[0], recv_sem=last.at[1], device_id=pair, device_id_type=MESH)
    done = set()
    swapped = False
    for key in TASK_ORDER:
        if key[0] == "pair":
            remote(key).start()
            continue
        if not swapped:
            swap.start()
            swapped = True
        for dep in sorted(TASKS[key]["deps"], key=lambda k: DONE_AT[k]):
            if dep[0] == "sum" or dep in done:
                continue
            if dep[0] == "pair":
                loads[dep[1]].wait()
            remote(dep).wait_recv()
            done.add(dep)
        work(key)
        if key[0] == "send":
            remote(key).start()
    keep = pltpu.make_async_copy(total, grad_out.at[:, pl.ds(row_mine, 64), :], last.at[2])
    give = pltpu.make_async_remote_copy(
        src_ref=total, dst_ref=grad_out.at[:, pl.ds(row_mine, 64), :], send_sem=last.at[3], recv_sem=last.at[4],
        device_id=pair, device_id_type=MESH)
    keep.start()
    give.start()
    for key in SEND_INDEX:
        if key not in done:
            if key[0] == "pair":
                loads[key[1]].wait()
            remote(key).wait_recv()
        remote(key).wait_send()
    swap.wait()
    keep.wait()
    give.wait()


def reduce_parts(slots, used, user_part, cid=1, name='reduce_parts'):
    scratch = [pltpu.VMEM((8, 4, 4, 64, 256), jnp.bfloat16)] * 2
    for i in range(3):
        kk, rows, (na, nb, nc) = dims(i)
        unit = (kk, rows, 256)
        scratch += [pltpu.VMEM((nb, 2, nc // 2, na) + unit, jnp.bfloat16)] * 2
        scratch += [pltpu.VMEM((nb, na) + unit, jnp.float32)]
        scratch += [pltpu.VMEM((2, nb // 2, na) + unit, jnp.bfloat16)] * 2
        scratch += [pltpu.VMEM((na,) + unit, jnp.float32)]
        scratch += [pltpu.VMEM((2, na // 2) + unit, jnp.float32)] * 2
    count = len(SEND_INDEX)
    scratch += [
        pltpu.VMEM((2, 64, 256), jnp.float32),
        pltpu.SemaphoreType.DMA((count,)), pltpu.SemaphoreType.DMA((count,)),
        pltpu.SemaphoreType.DMA((8,)), pltpu.SemaphoreType.DMA((5,)),
    ]
    anywhere = pl.BlockSpec(memory_space=pl.ANY)
    return pl.pallas_call(
        reduce_kernel,
        out_shape=(
            jax.ShapeDtypeStruct(user_part.shape, jnp.float32),
            jax.ShapeDtypeStruct((2, 128, 256), jnp.float32),
        ),
        in_specs=[anywhere, pl.BlockSpec(memory_space=pltpu.SMEM), anywhere],
        out_specs=(anywhere, anywhere),
        scratch_shapes=scratch,
        name=name,
        compiler_params=pltpu.CompilerParams(collective_id=cid, has_side_effects=True, vmem_limit_bytes=56 * 2**20),
    )(slots.reshape(8, 4, 4, 128, 256), used, user_part)


GROUP, RING = 16, 32


def tiles_kernel(keys_ref, panels_ref, counts_ref, users_ref, slots_out, user_out, half, raw, usem, vbuf, cbuf, acc, stage, vsem, csem, ssem):
    tiles = counts_ref.shape[0]

    def key(i):
        return keys_ref[jnp.clip(i, 0, tiles - 1)]

    def owner(i):
        return lax.shift_right_logical(key(i), 11)

    def fetch(i):
        k = key(i)
        slot = lax.rem(i, RING)
        item = lax.shift_right_logical(k, 10)
        tile = lax.rem(lax.shift_right_logical(k, 3), 128)
        return (
            pltpu.make_async_copy(panels_ref.at[item], vbuf.at[slot], vsem.at[slot]),
            pltpu.make_async_copy(counts_ref.at[tile], cbuf.at[slot], csem.at[slot]),
        )

    def put(i):
        slot = lax.rem(i, RING)
        return pltpu.make_async_copy(stage.at[slot], slots_out.at[owner(i)], ssem.at[slot])

    def is_last(i):
        return (i == tiles - 1) | (owner(i) != owner(i + 1))

    def start(i, _):
        for c in fetch(i):
            c.start()
        return 0

    bring = pltpu.make_async_copy(users_ref, raw, usem)
    bring.start()
    lax.fori_loop(0, RING, start, 0)
    bring.wait()
    half[...] = raw[...].astype(jnp.bfloat16)
    user_out[...] = jnp.zeros_like(user_out)
    acc[...] = jnp.zeros_like(acc)

    def group(g, _):
        base = g * GROUP
        for n in range(GROUP):
            for c in fetch(base + n):
                c.wait()

        @pl.when(base >= RING)
        def _():
            for n in range(GROUP):

                @pl.when(is_last(base + n - RING))
                def _():
                    put(base + n - RING).wait()

        errs = []
        for n in range(GROUP):
            i = base + n
            slot = lax.rem(i, RING)
            block = lax.rem(key(i), 8)
            u = half[block]
            v = vbuf[slot]
            predicted = lax.dot_general(u, v, (((1,), (1,)), ((), ())), preferred_element_type=jnp.float32)
            amount = cbuf[slot].astype(jnp.float32)
            weight = amount * (0.5 / 64.0) + 1.0 / 64.0
            errs.append((weight * (predicted - jnp.where(amount > 0, 1.0, 0.0))).astype(jnp.bfloat16))
        for n in range(GROUP):
            i = base + n
            slot = lax.rem(i, RING)
            block = lax.rem(key(i), 8)
            first = (i == 0) | (owner(i) != owner(i - 1))
            item_part = lax.dot_general(errs[n], half[block], (((0,), (0,)), ((), ())), preferred_element_type=jnp.float32)
            total = jnp.where(first, 0.0, acc[...]) + item_part
            acc[...] = total
            stage[slot] = total.astype(jnp.bfloat16)
            user_out[block] += jnp.dot(errs[n], vbuf[slot], preferred_element_type=jnp.float32)
        for n in range(GROUP):
            i = base + n

            @pl.when(is_last(i))
            def _():
                put(i).start()

        @pl.when(base + RING < tiles)
        def _():
            for n in range(GROUP):
                for c in fetch(base + n + RING):
                    c.start()

        return 0

    lax.fori_loop(0, tiles // GROUP, group, 0)

    def finish(n, _):
        i = tiles - RING + n

        @pl.when(is_last(i))
        def _():
            put(i).wait()

        return 0

    lax.fori_loop(0, RING, finish, 0)


def tile_parts(keys, panels, counts, users):
    anywhere = pl.BlockSpec(memory_space=pl.ANY)
    whole = pl.BlockSpec(memory_space=pltpu.VMEM)
    return pl.pallas_call(
        tiles_kernel,
        out_shape=(
            jax.ShapeDtypeStruct((128, 128, 256), jnp.bfloat16),
            jax.ShapeDtypeStruct((8, 128, 256), jnp.float32),
        ),
        in_specs=[pl.BlockSpec(memory_space=pltpu.SMEM), anywhere, anywhere, anywhere],
        out_specs=(anywhere, whole),
        scratch_shapes=[
            pltpu.VMEM((8, 128, 256), jnp.bfloat16),
            pltpu.VMEM((8, 128, 256), jnp.float32),
            pltpu.SemaphoreType.DMA,
            pltpu.VMEM((RING, 128, 256), jnp.bfloat16),
            pltpu.VMEM((RING, 128, 128), jnp.bfloat16),
            pltpu.VMEM((128, 256), jnp.float32),
            pltpu.VMEM((RING, 128, 256), jnp.bfloat16),
            pltpu.SemaphoreType.DMA((RING,)),
            pltpu.SemaphoreType.DMA((RING,)),
            pltpu.SemaphoreType.DMA((RING,)),
        ],
        name="tile_parts",
        compiler_params=pltpu.CompilerParams(vmem_limit_bytes=58 * 2**20),
        cost_estimate=pl.CostEstimate(flops=128 * 6 * 128 * 128 * 256, bytes_accessed=26 * 2**20, transcendentals=0),
    )(keys, panels, counts, users)


def adagrad_kernel(part, other, users, user_accum, grad, items, item_accum, new_users, new_user_accum, new_items, new_item_accum):
    for g, factors, accum, new, new_accum in (
        (part[...] + other[...], users, user_accum, new_users, new_user_accum),
        (grad[...], items, item_accum, new_items, new_item_accum),
    ):
        total = accum[...] + g * g
        new_accum[...] = total
        new[...] = factors[...] - g / jnp.sqrt(total)


def adagrad(part, other, users, user_accum, grad, items, item_accum, steps=2):
    def rows(x):
        return pl.BlockSpec((x.shape[0] // steps, x.shape[1]), lambda n: (n, 0))

    args = (part, other, users, user_accum, grad, items, item_accum)
    outs = (users, user_accum, items, item_accum)
    return pl.pallas_call(
        adagrad_kernel,
        grid=(steps,),
        out_shape=tuple(jax.ShapeDtypeStruct(x.shape, x.dtype) for x in outs),
        in_specs=[rows(x) for x in args],
        out_specs=tuple(rows(x) for x in outs),
        name="adagrad",
        compiler_params=pltpu.CompilerParams(vmem_limit_bytes=56 * 2**20),
    )(*args)


def local(user_factors, user_accum, item_factors, item_accum, tile_counts, tile_user, tile_item, send_list):
    counts = tile_counts[0, 0]
    panels, keys, used = gather_panels(item_factors, tile_item[0], tile_user[0])
    slots, user_part = tile_parts(keys[0], panels.reshape(256, 128, 256), counts, user_factors.reshape(8, 128, 256))
    other_user, item_grad = reduce_parts(slots, used, user_part.reshape(1024, 256))
    return adagrad(
        user_part.reshape(1024, 256), other_user, user_factors, user_accum,
        item_grad.reshape(256, 256), item_factors, item_accum,
    )


def solution(mesh):
    rows = P("users", None)
    return jax.shard_map(
        local,
        mesh=mesh,
        in_specs=(rows, rows, rows, rows, P("users", "rep", None, None, None), P("users", "rep", None), P("users", "rep", None), P("users", "rep", None)),
        out_specs=(rows, rows, rows, rows),
        check_vma=False,
    )
```
